32 devices in a mesh: row: 4 (over y, x), col: 8 (over z, core).
Axes of the slice: x: 2, y: 2, z: 4, core: 2. Of those that a mesh axis runs over, the one named last changes fastest.
Arguments:
- allele_doses: int32 [4096, 65536], P('row', 'col'), may hold values from 0 to 2
- disease_status: int32 [4096], P('row'), may hold values from 0 to 1
- walker_cloud: float32 [64, 65536], P(None, 'col'), may hold values from -21 to 21
- normal_perturbations: float32 [2, 64, 65536], P(None, None, 'col'), may hold values from -6 to 6
- approval_flags: int32 [2, 64], replicated, may hold values 0 or 1
- present_heat: float32 [1], replicated, may hold values from 0.85 to 0.92
- heat_advance: float32 [1], replicated, may hold values from 0.02 to 0.08
- drift_magnitude: float32 [1], replicated, may hold values from 0.8 to 1.2
Outputs:
- particles_out: float32 [64, 65536], P(None, 'col')
- log_weights: float32 [64], replicated
- mean_loglik: float32 [64], replicated
The draws below stay inside these ranges and needn't reach their ends.
All inputs are finite; a program needn't handle non-finite values.
Results may differ from the reference program's by a relative error of at most 0.0035.
Values may be sent and summed in bfloat16 or wider, within the bound.
No kernel may reach another device: no remote copies, remote signals or barrier semaphores. Data moves between devices by JAX's collectives and lax.ppermute only.
A program may use at most 128 MiB of HBM per device.

```python
import math
import jax
import jax.numpy as jnp
from jax import lax

P_SIZE = 65536
K = 64
N = 4096
N_ROW = 4


def draw_walker_cloud(key, part):
    first, second = jax.random.split(jax.random.fold_in(key, 7301), 2)
    particle_location = jnp.arange(P_SIZE, dtype=jnp.float32) / float(P_SIZE - 1)
    column_scale = jnp.exp(jnp.log(3.0) * particle_location) * jax.random.uniform(second, (P_SIZE,), jnp.float32, 0.7, 1.4)
    base = jax.random.normal(first, (K, P_SIZE), jnp.float32)
    base = jnp.clip(base, -5.0, 5.0)
    return base * column_scale[None, :]


def plant(drawn, stream_key, least, top_value):
    extent = drawn.shape
    index_at = [jax.random.randint(jax.random.fold_in(stream_key, axis), (), 0, extent[axis]) for axis in range(len(extent))]
    drawn = drawn.at[tuple(index_at)].set(least)
    longest = extent.index(max(extent))
    index_at[longest] = (index_at[longest] + 1) % extent[longest]
    return drawn.at[tuple(index_at)].set(top_value)


def block_levels(own_key, extent, shards, smallest, high):
    gain = 1.0
    for axis_at, blocks in shards:
        steps = jax.random.uniform(jax.random.fold_in(jax.random.fold_in(own_key, 6), axis_at), (blocks,), jnp.float32, smallest / len(shards), high / len(shards))
        gain = gain * jnp.repeat(jnp.exp(steps), extent[axis_at] // blocks).reshape((-1,) + (1,) * (len(extent) - 1 - axis_at))
    return gain


def bell_draw(own_key, shape, deviation, limit, cuts=(), kind=jnp.bfloat16):
    values = jax.random.normal(own_key, shape, jnp.float32) * deviation
    if len(cuts) > 0:
        values = block_levels(own_key, shape, cuts, -0.22, 0.18) * values
    return jnp.clip(values, min=-limit, max=limit).astype(kind)


def setup_inputs(seed: int = 0) -> dict:
    keys = jax.random.split(jax.random.key(seed), 9)
    allele_doses = plant(jax.random.randint(keys[0], (N, P_SIZE), 0, 3), jax.random.fold_in(keys[0], 1), 0, 2).astype(jnp.int32)
    disease_status = plant(jax.random.randint(keys[1], (N,), 0, 2), jax.random.fold_in(keys[1], 1), 0, 1).astype(jnp.int32)
    walker_cloud = draw_walker_cloud(jax.random.fold_in(keys[8], 71), 0)
    normal_perturbations = bell_draw(keys[3], (2, K, P_SIZE), 1.0, 6.0, ((2, 8),), jnp.float32)
    approval_flags = plant((jax.random.randint(keys[4], (2, K), 0, 4) < 3).astype(jnp.int32), jax.random.fold_in(keys[4], 1), 0, 1)
    present_heat = jnp.clip(jax.random.uniform(keys[5], (1,), jnp.float32, 0.85, 0.92), 0.85, 0.92)
    heat_advance = jnp.clip(jnp.exp(jax.random.uniform(keys[6], (1,), jnp.float32, math.log(0.02), math.log(0.08))), 0.02, 0.08)
    drift_magnitude = jnp.clip(jnp.exp(jax.random.uniform(keys[7], (1,), jnp.float32, math.log(0.8), math.log(1.2))), 0.8, 1.2)
    return {"allele_doses": allele_doses, "disease_status": disease_status, "walker_cloud": walker_cloud, "normal_perturbations": normal_perturbations, "approval_flags": approval_flags, "present_heat": present_heat, "heat_advance": heat_advance, "drift_magnitude": drift_magnitude}


CLIP_FLOOR = 4.0
SHRINKAGE_LEVEL = 0.5

def logits_of(allele_doses, regression_weight):
    reciprocal_square = float(P_SIZE) ** (-0.5)
    coef_bf = regression_weight.astype(jnp.bfloat16)
    blocks = allele_doses.reshape(N_ROW, -1, P_SIZE)

    def single_block_result(block):
        centered = (block - 1).astype(jnp.bfloat16)
        return jnp.dot(centered, coef_bf.T, preferred_element_type=jnp.float32)
    return lax.map(single_block_result, blocks).reshape(-1, K) * reciprocal_square

def likgrad_of(allele_doses, residual_bf):
    blocks = allele_doses.reshape(N_ROW, -1, P_SIZE)
    residual_block_list = residual_bf.reshape(N_ROW, -1, K)

    def single_block_result(pair):
        centered = (pair[0] - 1).astype(jnp.bfloat16)
        partial_sum = jnp.dot(pair[1].T, centered, preferred_element_type=jnp.float32)
        rounded = lax.optimization_barrier(partial_sum.astype(jnp.bfloat16))
        return rounded.astype(jnp.float32)
    return lax.optimization_barrier(jnp.sum(lax.map(single_block_result, (blocks, residual_block_list)), axis=0))

def loglik_of(outcome, linear_predictor):
    return lax.optimization_barrier(jnp.sum(outcome[:, None] * linear_predictor - jax.nn.softplus(linear_predictor), axis=0))

def reference(allele_doses, disease_status, walker_cloud, normal_perturbations, approval_flags, present_heat, heat_advance, drift_magnitude):
    reciprocal_square = float(P_SIZE) ** (-0.5)
    outcome = disease_status.astype(jnp.float32)
    upcoming_heat = present_heat[0] + heat_advance[0]
    stepped = drift_magnitude[0]
    linear_predictor = logits_of(allele_doses, walker_cloud)
    loglik = loglik_of(outcome, linear_predictor)
    scaled = heat_advance[0] * loglik
    clipped = jnp.maximum(scaled - jnp.max(scaled), -CLIP_FLOOR)
    log_weights = clipped - jnp.log(jnp.sum(jnp.exp(clipped)))
    weights = jnp.exp(log_weights)
    center = lax.optimization_barrier(jnp.sum(weights[:, None] * walker_cloud, axis=0))
    spread = lax.optimization_barrier(jnp.sum(weights[:, None] * (walker_cloud - center[None, :]) ** 2, axis=0)) + 1e-06
    precond = spread / (jnp.sum(spread) / P_SIZE)
    regression_weight = walker_cloud
    for move in range(2):
        residual_bf = (outcome[:, None] - jax.nn.sigmoid(linear_predictor)).astype(jnp.bfloat16)
        fitness_slope = likgrad_of(allele_doses, residual_bf)
        slope_vector = upcoming_heat * reciprocal_square * fitness_slope - SHRINKAGE_LEVEL * regression_weight / jnp.sqrt(regression_weight * regression_weight + 1.0)
        proposal = regression_weight + stepped * precond[None, :] * slope_vector + jnp.sqrt(2.0 * stepped * precond)[None, :] * normal_perturbations[move]
        regression_weight = jnp.where(approval_flags[move][:, None] == 1, proposal, regression_weight)
        linear_predictor = logits_of(allele_doses, regression_weight)
    mean_loglik = loglik_of(outcome, linear_predictor) / (P_SIZE * 0 + allele_doses.shape[0])
    return (regression_weight, log_weights, mean_loglik)
```

```python
import functools

import jax
import jax.numpy as jnp
from jax import lax
from jax.experimental import pallas as pl
from jax.experimental.pallas import tpu as pltpu
from jax.sharding import PartitionSpec as P

CLIP_FLOOR = 4.0
SHRINKAGE_LEVEL = 0.5
F32 = jnp.float32
BF16 = jnp.bfloat16
VMEM = pl.BlockSpec(memory_space=pltpu.VMEM)
SMEM = pl.BlockSpec(memory_space=pltpu.SMEM)
HBM = pl.BlockSpec(memory_space=pltpu.HBM)
MIB = 1 << 20
LANES = 128
CHUNKS = 2
PIECES = 2


def rows_dot(left, right):
    return lax.dot_general(left, right, (((1,), (1,)), ((), ())), preferred_element_type=F32)


def tile_of(size, most):
    while size % most:
        most //= 2
    return most


def params(mib):
    return pltpu.CompilerParams(vmem_limit_bytes=mib * MIB)


def cost(flops):
    return pl.CostEstimate(flops=flops, bytes_accessed=0, transcendentals=0)


def as_lanes(value):
    high = value.astype(BF16)
    rest = value - high.astype(F32)
    middle = rest.astype(BF16)
    low = (rest - middle.astype(F32)).astype(BF16)
    lane = lax.broadcasted_iota(jnp.int32, (value.shape[0], LANES), 1)
    zero = jnp.zeros((value.shape[0], LANES), F32)
    out = jnp.where(lane == 0, high.astype(F32), zero)
    out = jnp.where(lane == 1, middle.astype(F32), out)
    return jnp.where(lane == 2, low.astype(F32), out).astype(BF16)


def flipped(value):
    size = max(value.shape)
    diagonal = lax.broadcasted_iota(jnp.int32, (size, size), 0) == lax.broadcasted_iota(
        jnp.int32, (size, size), 1
    )
    return jnp.sum(
        jnp.where(diagonal, value, 0.0), axis=int(value.shape[0] == 1), keepdims=True
    )


def from_lanes(lanes):
    return jnp.sum(lanes.astype(F32), axis=1, keepdims=True)


def center_kernel(block, with_gram, core, doses, cloud, centered, mine, other, cloud_bf, logits, gram):
    step = pl.program_id(0)
    variants = doses.shape[1]
    people = logits.shape[1]
    half = people // 2

    @pl.when(step == 0)
    def _():
        cloud_bf[...] = cloud[...].astype(BF16)

    if with_gram:

        @pl.when(step == 0)
        def _():
            width = tile_of(variants, 1024)
            total = None
            for start in range(0, variants, width):
                c = cloud[:, start : start + width]
                c = c - jnp.mean(c, axis=0, keepdims=True)
                high = c.astype(BF16)
                low = (c - high.astype(F32)).astype(BF16)
                term = rows_dot(high, high) + 2.0 * rows_dot(high, low)
                total = term if total is None else total + term
            gram[...] = jnp.zeros(gram.shape, F32)
            gram[:, : total.shape[1]] = total

    width = tile_of(variants, 2048)
    total = None
    for start in range(0, variants, width):
        part = (doses[:, start : start + width] - 1).astype(F32).astype(BF16)
        centered[pl.ds(pl.multiple_of(step * block, block), block), start : start + width] = part
        term = rows_dot(part, cloud_bf[:, start : start + width])
        total = term if total is None else total + term
    logits[:, pl.ds(pl.multiple_of(step * block, block), block)] = total.T

    @pl.when(step == pl.num_programs(0) - 1)
    def _():
        first = core[0]
        mine[:, :half] = logits[:, pl.ds(pl.multiple_of(first * half, half), half)]
        other[:, :half] = logits[:, pl.ds(pl.multiple_of((1 - first) * half, half), half)]
        if with_gram:
            mine[:, half:] = gram[...]
            other[:, half:] = gram[...]


def center_and_first_logits(chunk, core, doses, cloud):
    variants = doses.shape[1]
    people = doses.shape[0] // CHUNKS
    particles = cloud.shape[0]
    block = min(256, people)
    steps = people // block
    with_gram = chunk == 0
    lanes = people // 2 + (LANES if with_gram else 0)
    exchanged = jax.ShapeDtypeStruct((particles, lanes), F32)
    return pl.pallas_call(
        functools.partial(center_kernel, block, with_gram),
        grid=(steps,),
        in_specs=[
            SMEM,
            pl.BlockSpec((block, variants), lambda i: (chunk * steps + i, 0)),
            pl.BlockSpec((particles, variants), lambda i: (0, 0), pipeline_mode=pl.Buffered(1)),
        ],
        out_specs=[VMEM, VMEM, VMEM],
        out_shape=[pltpu.VMEM((people, variants), BF16), exchanged, exchanged],
        scratch_shapes=[
            pltpu.VMEM((particles, variants), BF16),
            pltpu.VMEM((particles, people), F32),
            pltpu.VMEM((particles, LANES), F32),
        ],
        compiler_params=params(28),
        cost_estimate=cost(16 * particles * people * variants),
        name="center_and_first_logits",
    )(core, doses, cloud)


def residual_kernel(parts, people, chunks, scale, earlier, tail, gram, loglik_as, core, status, *refs):
    sent, refs = refs[:parts], list(refs[parts:])
    before = refs.pop(0) if earlier else None
    half = people // 2
    outcome = jnp.concatenate(
        [
            status[:, pl.ds(pl.multiple_of(chunk * people + core[0] * half, half), half)]
            for chunk in chunks
        ],
        axis=1,
    ).astype(F32)
    share = half * len(chunks)
    values = tree_sum([ref[...].astype(F32) for ref in sent])
    logits = values[:, :share] * scale
    residual = refs.pop(0)
    residual[:, :share] = (outcome - jax.nn.sigmoid(logits)).astype(BF16)
    if loglik_as or tail:
        softplus = jnp.maximum(logits, 0.0) + jnp.log1p(jnp.exp(-jnp.abs(logits)))
        loglik = jnp.sum(outcome * logits - softplus, axis=1, keepdims=True)
        if earlier:
            loglik = loglik + before[...]
        if tail:
            residual[:, share:] = as_lanes(loglik)
        if loglik_as:
            refs.pop(0)[...] = loglik if loglik_as == "column" else flipped(loglik)
    if gram:
        refs.pop(0)[...] = values[:, share:]


def residual_of(scale, core, status, chunks, sent, earlier=None, tail=False, gram=False, loglik_as=None):
    particles = sent[0].shape[0]
    people = status.shape[1] // CHUNKS
    share = people // 2 * len(chunks)
    out_shape = [jax.ShapeDtypeStruct((particles, share + (LANES if tail else 0)), BF16)]
    if loglik_as:
        shape = (particles, 1) if loglik_as == "column" else (1, particles)
        out_shape.append(jax.ShapeDtypeStruct(shape, F32))
    if gram:
        out_shape.append(jax.ShapeDtypeStruct((particles, LANES), F32))
    operands = [core, status, *sent] + ([earlier] if earlier is not None else [])
    return pl.pallas_call(
        functools.partial(
            residual_kernel, len(sent), people, chunks, scale, earlier is not None, tail, gram, loglik_as
        ),
        in_specs=[SMEM] + [VMEM] * (len(operands) - 1),
        out_specs=[VMEM] * len(out_shape),
        out_shape=out_shape,
        compiler_params=params(12),
        name="residual",
    )(*operands)


def gradient_kernel(count, first, columns, tail, core, *refs):
    pairs, centered = refs[: 2 * count], refs[2 * count : 2 * count + CHUNKS]
    grad, residual = refs[2 * count + CHUNKS :]
    people = centered[0].shape[0]
    half = people // 2
    mine = core[0]
    for chunk in range(CHUNKS):
        own, other = (pairs[2 * chunk], pairs[2 * chunk + 1]) if count == CHUNKS else pairs
        at = 0 if count == CHUNKS else chunk * half
        base = chunk * people
        residual[:, pl.ds(pl.multiple_of(base + mine * half, half), half)] = own[:, at : at + half]
        residual[:, pl.ds(pl.multiple_of(base + (1 - mine) * half, half), half)] = other[
            :, at : at + half
        ]
    width = tile_of(columns, 512)
    for start in range(0, columns, width):
        here = slice(first + start, first + start + width)
        grad[:, start : start + width] = sum(
            jnp.dot(
                residual[:, chunk * people : (chunk + 1) * people],
                centered[chunk][:, here],
                preferred_element_type=F32,
            )
            for chunk in range(CHUNKS)
        ).astype(BF16)
    if tail:
        grad[:, columns:] = as_lanes(from_lanes(own[:, half:]) + from_lanes(other[:, half:]))


def gradient(first, columns, tail, core, pairs, centered):
    particles = pairs[0].shape[0]
    people = sum(c.shape[0] for c in centered)
    return pl.pallas_call(
        functools.partial(gradient_kernel, len(pairs) // 2, first, columns, tail),
        in_specs=[SMEM] + [VMEM] * (len(pairs) + CHUNKS),
        out_specs=VMEM,
        out_shape=jax.ShapeDtypeStruct((particles, columns + (LANES if tail else 0)), BF16),
        scratch_shapes=[pltpu.VMEM((particles, people), BF16)],
        compiler_params=params(8),
        cost_estimate=cost(8 * particles * people * columns),
        name="gradient",
    )(core, *pairs, *centered)


def pair_sum_kernel(columns, tail, left, right, out):
    total = left[:, :columns].astype(F32) + right[:, :columns].astype(F32)
    out[:, :columns] = total.astype(BF16)
    if tail:
        out[:, columns:] = as_lanes(from_lanes(left[:, columns:]) + from_lanes(right[:, columns:]))


def pair_sum(columns, tail, left, right):
    return pl.pallas_call(
        functools.partial(pair_sum_kernel, columns, tail),
        in_specs=[VMEM, VMEM],
        out_specs=VMEM,
        out_shape=jax.ShapeDtypeStruct(left.shape, BF16),
        compiler_params=params(8),
        name="pair_sum",
    )(left, right)


def weigh(total_variants, heat_advance, loglik, gram):
    scaled = heat_advance * loglik
    clipped = jnp.maximum(scaled - jnp.max(scaled, axis=0, keepdims=True), -CLIP_FLOOR)
    log_weights = clipped - jnp.log(jnp.sum(jnp.exp(clipped), axis=0, keepdims=True))
    weights = jnp.exp(log_weights)
    particles = loglik.shape[0]
    gram = gram[:, :particles]
    diagonal = lax.broadcasted_iota(jnp.int32, gram.shape, 0) == lax.broadcasted_iota(
        jnp.int32, gram.shape, 1
    )
    square = jnp.sum(jnp.where(diagonal, gram * weights, 0.0), axis=0, keepdims=True)
    mixed = jnp.sum(weights * gram, axis=0, keepdims=True) * flipped(weights)
    total = jnp.sum(square - mixed, axis=1, keepdims=True)
    return log_weights, weights, total / total_variants + 1e-06


def update_kernel(first, move, total_variants, core, old_heat, advance, drift_ref, flags, cloud, noise, *refs):
    known, refs = refs[0], refs[1:]
    centered, refs = refs[:CHUNKS], refs[CHUNKS:]
    grads, refs = refs[: 2 * PIECES], list(refs[2 * PIECES :])
    moved, mine, other = refs[:3]
    refs = refs[3:]
    if first:
        log_weights_out, size_out = refs[:2]
        refs = refs[2:]
    c_buffer, noise_buffer, total, in_sems, out_sems = refs
    particles, variants = cloud.shape
    people = centered[0].shape[0]
    width = tile_of(variants // PIECES, 2048)
    steps = variants // width

    def load(step):
        here = pl.ds(step * width, width)
        return (
            pltpu.make_async_copy(cloud.at[:, here], c_buffer.at[:, here], in_sems.at[0, step]),
            pltpu.make_async_copy(noise.at[move, :, here], noise_buffer.at[:, here], in_sems.at[1, step]),
        )

    def store(step):
        here = pl.ds(step * width, width)
        return pltpu.make_async_copy(c_buffer.at[:, here], moved.at[:, here], out_sems.at[step])

    for step in range(steps):
        for copy in load(step):
            copy.start()
    heat = (old_heat[0] + advance[0]) * float(total_variants) ** (-0.5)
    drift = drift_ref[0]
    approved = flipped(flags[move : move + 1, :].astype(F32)) > 0.5
    columns = variants // PIECES
    if first:
        loglik = from_lanes(grads[0][:, columns:]) + from_lanes(grads[1][:, columns:])
        log_weights, weights, mean_spread = weigh(total_variants, advance[0], loglik, known[...])
        log_weights_out[...] = flipped(log_weights)
        factor = drift / mean_spread
    for step in range(steps):
        piece, begin = divmod(step * width, columns)
        for copy in load(step):
            copy.wait()
        chosen = []
        narrow = tile_of(width, 512)
        for start in range(step * width, (step + 1) * width, narrow):
            here = slice(start, start + narrow)
            local = slice(start - piece * columns, start - piece * columns + narrow)
            c = c_buffer[:, here]
            if first:
                center = jnp.sum(weights * c, axis=0, keepdims=True)
                spread = jnp.sum(weights * (c - center) ** 2, axis=0, keepdims=True) + 1e-06
                size = spread * factor
                size_out[:, here] = size
            else:
                size = known[:, here]
            slope = grads[2 * piece][:, local].astype(F32) + grads[2 * piece + 1][:, local].astype(F32)
            rise = heat * slope - SHRINKAGE_LEVEL * c * lax.rsqrt(c * c + 1.0)
            proposal = c + size * rise + jnp.sqrt(2.0 * size) * noise_buffer[:, here]
            c = jnp.where(approved, proposal, c)
            c_buffer[:, here] = c
            chosen.append(c.astype(BF16))
        store(step).start()
        chosen = jnp.concatenate(chosen, axis=1)
        for chunk in range(CHUNKS):
            rows = slice(chunk * people, (chunk + 1) * people)
            term = rows_dot(centered[chunk][:, step * width : (step + 1) * width], chosen)
            total[rows, :] = term if step == 0 else total[rows, :] + term
    half = people // 2
    here = core[0]
    for chunk in range(CHUNKS):
        out = slice(chunk * half, (chunk + 1) * half)
        base = chunk * people
        mine[:, out] = total[pl.ds(pl.multiple_of(base + here * half, half), half), :].T
        other[:, out] = total[pl.ds(pl.multiple_of(base + (1 - here) * half, half), half), :].T
    for step in range(steps):
        store(step).wait()


def update_and_logits(first, move, total_variants, core, scalars, flags, cloud, noise, known, centered, grads):
    particles, variants = cloud.shape
    people = sum(c.shape[0] for c in centered)
    steps = variants // tile_of(variants // PIECES, 2048)
    exchanged = jax.ShapeDtypeStruct((particles, people // 2), F32)
    out_shape = [jax.ShapeDtypeStruct((particles, variants), F32), exchanged, exchanged]
    if first:
        out_shape.append(jax.ShapeDtypeStruct((1, particles), F32))
        out_shape.append(jax.ShapeDtypeStruct((1, variants), F32))
    return pl.pallas_call(
        functools.partial(update_kernel, first, move, total_variants),
        in_specs=[SMEM] * 4 + [VMEM, HBM, HBM] + [VMEM] * (1 + CHUNKS + len(grads)),
        out_specs=[HBM] + [VMEM] * (len(out_shape) - 1),
        out_shape=out_shape,
        scratch_shapes=[
            pltpu.VMEM((particles, variants), F32),
            pltpu.VMEM((particles, variants), F32),
            pltpu.VMEM((people, particles), F32),
            pltpu.SemaphoreType.DMA((2, steps)),
            pltpu.SemaphoreType.DMA((steps,)),
        ],
        compiler_params=params(16),
        cost_estimate=cost(8 * particles * people * variants),
        name="update_and_logits",
    )(core, *scalars, flags, cloud, noise, known, *centered, *grads)


def swap(value, axis, distance):
    size = lax.axis_size(axis)
    return lax.ppermute(value, axis, [(i, i ^ distance) for i in range(size)])


def tree_sum(values):
    values = list(values)
    while len(values) > 1:
        values = [values[i] + values[i + 1] for i in range(0, len(values), 2)]
    return values[0]


def over_chips(mine, other, link):
    mine = (mine + swap(other, "col", 1)).astype(link)
    return [mine] + [swap(mine, "col", d) for d in range(2, lax.axis_size("col"), 2)]


def sum_small(value):
    value = value + swap(value, "col", 1)
    size = lax.axis_size("row")
    return tree_sum([value] + [swap(value, "row", d) for d in range(1, size)])


def local(
    allele_doses,
    disease_status,
    walker_cloud,
    normal_perturbations,
    approval_flags,
    present_heat,
    heat_advance,
    drift_magnitude,
):
    people, variants = allele_doses.shape
    total_variants = variants * lax.axis_size("col")
    total_people = people * lax.axis_size("row")
    scale = float(total_variants) ** (-0.5)
    core = lax.axis_index("col") % 2
    core_ref = core.reshape(1)
    status = disease_status.reshape(1, people)
    scalars = (present_heat, heat_advance, drift_magnitude)
    row_bits = [1 << b for b in range(lax.axis_size("row").bit_length() - 1)]

    centered, pairs, loglik, gram = [], [], None, None
    for chunk in range(CHUNKS):
        part, mine, other = center_and_first_logits(chunk, core_ref, allele_doses, walker_cloud)
        centered.append(part)
        sent = over_chips(mine, other, F32)
        tail = chunk == CHUNKS - 1
        own, *extra = residual_of(
            scale,
            core_ref,
            status,
            (chunk,),
            sent,
            earlier=loglik,
            tail=tail,
            gram=chunk == 0,
            loglik_as=None if tail else "column",
        )
        if chunk == 0:
            gram = extra.pop()
        if not tail:
            (loglik,) = extra
        pairs += [own, swap(own, "col", 1)]

    moved, known = walker_cloud, gram
    columns = variants // PIECES
    for move in range(2):
        first = move == 0
        grads = []
        for piece in range(PIECES):
            tail = first and piece == 0
            grad = gradient(piece * columns, columns, tail, core_ref, pairs, centered)
            order = row_bits if piece % 2 == 0 else row_bits[::-1]
            for bit in order[:-1]:
                grad = pair_sum(columns, tail, grad, swap(grad, "row", bit))
            grads += [grad, swap(grad, "row", order[-1])]
        moved, mine, other, *extra = update_and_logits(
            first,
            move,
            total_variants,
            core_ref,
            scalars,
            approval_flags,
            moved,
            normal_perturbations,
            known,
            centered,
            grads,
        )
        if first:
            log_weights, known = extra
        sent = over_chips(mine, other, BF16)
        if first:
            (own,) = residual_of(scale, core_ref, status, tuple(range(CHUNKS)), sent)
            pairs = [own, swap(own, "col", 1)]
        else:
            _, loglik = residual_of(
                scale, core_ref, status, tuple(range(CHUNKS)), sent, loglik_as="row"
            )
    mean_loglik = sum_small(loglik) / total_people
    return (moved, log_weights[0], mean_loglik[0])


def solution(mesh):
    placed = (P("row", "col"), P("row"), P(None, "col"), P(None, None, "col"), P(), P(), P(), P())
    return jax.shard_map(
        local, mesh=mesh, in_specs=placed, out_specs=(P(None, "col"), P(), P()), check_vma=False
    )
```

```python
import functools

import jax
import jax.numpy as jnp
from jax import lax
from jax.experimental import pallas as pl
from jax.experimental.pallas import tpu as pltpu
from jax.sharding import PartitionSpec as P

CLIP_FLOOR = 4.0
SHRINKAGE_LEVEL = 0.5
F32 = jnp.float32
BF16 = jnp.bfloat16
VMEM = pl.BlockSpec(memory_space=pltpu.VMEM)
SMEM = pl.BlockSpec(memory_space=pltpu.SMEM)
HBM = pl.BlockSpec(memory_space=pltpu.HBM)
KEEP, SEND = 0, 1
MIB = 1 << 20
LANES = 128
CHUNKS = 1
PIECES = 4


def core_of():
    return lax.rem(lax.axis_index("col"), 2)


def row_bits():
    return [1 << b for b in range(lax.axis_size("row").bit_length() - 1)]


def half_of(which, piece, variants):
    columns = variants // PIECES
    bits = row_bits()
    bit = jnp.where(lax.rem(jnp.int32(piece), 2) == 0, bits[0], bits[-1])
    own = lax.rem(lax.div(lax.axis_index("row"), bit), 2)
    chosen = own if which == KEEP else 1 - own
    return pl.multiple_of(piece * columns + chosen * (columns // 2), columns // 2)


def rows_dot(left, right):
    return lax.dot_general(left, right, (((1,), (1,)), ((), ())), preferred_element_type=F32)


def tile_of(size, most):
    while size % most:
        most //= 2
    return most


def params(mib):
    return pltpu.CompilerParams(vmem_limit_bytes=mib * MIB)


def cost(flops):
    return pl.CostEstimate(flops=flops, bytes_accessed=0, transcendentals=0)


def as_lanes(value):
    high = value.astype(BF16)
    rest = value - high.astype(F32)
    middle = rest.astype(BF16)
    low = (rest - middle.astype(F32)).astype(BF16)
    lane = lax.broadcasted_iota(jnp.int32, (value.shape[0], LANES), 1)
    zero = jnp.zeros((value.shape[0], LANES), F32)
    out = jnp.where(lane == 0, high.astype(F32), zero)
    out = jnp.where(lane == 1, middle.astype(F32), out)
    return jnp.where(lane == 2, low.astype(F32), out).astype(BF16)


def flipped(value):
    size = max(value.shape)
    diagonal = lax.broadcasted_iota(jnp.int32, (size, size), 0) == lax.broadcasted_iota(
        jnp.int32, (size, size), 1
    )
    return jnp.sum(
        jnp.where(diagonal, value, 0.0), axis=int(value.shape[0] == 1), keepdims=True
    )


def from_lanes(lanes):
    return jnp.sum(lanes.astype(F32), axis=1, keepdims=True)


def center_kernel(block, with_gram, doses, cloud, _, centered, mine, other, cloud_bf, logits, gram):
    step = pl.program_id(0)
    variants = doses.shape[1]
    people = logits.shape[1]
    half = people // 2

    @pl.when(step == 0)
    def _():
        cloud_bf[...] = cloud[...].astype(BF16)

    if with_gram:

        @pl.when(step == 0)
        def _():
            width = tile_of(variants, 1024)
            total = None
            for start in range(0, variants, width):
                c = cloud[:, start : start + width]
                c = c - jnp.mean(c, axis=0, keepdims=True)
                high = c.astype(BF16)
                low = (c - high.astype(F32)).astype(BF16)
                term = rows_dot(high, high) + 2.0 * rows_dot(high, low)
                total = term if total is None else total + term
            gram[...] = jnp.zeros(gram.shape, F32)
            gram[:, : total.shape[1]] = total

    width = tile_of(variants, 2048)
    total = None
    for start in range(0, variants, width):
        part = (doses[:, start : start + width] - 1).astype(F32).astype(BF16)
        centered[pl.ds(pl.multiple_of(step * block, block), block), start : start + width] = part
        term = rows_dot(part, cloud_bf[:, start : start + width])
        total = term if total is None else total + term
    logits[:, pl.ds(pl.multiple_of(step * block, block), block)] = total.T

    @pl.when(step == pl.num_programs(0) - 1)
    def _():
        first = core_of()
        mine[:, :half] = logits[:, pl.ds(pl.multiple_of(first * half, half), half)]
        other[:, :half] = logits[:, pl.ds(pl.multiple_of((1 - first) * half, half), half)]
        if with_gram:
            mine[:, half:] = gram[...]
            other[:, half:] = gram[...]


def center_and_first_logits(chunk, doses, cloud, scalars):
    variants = doses.shape[1]
    people = doses.shape[0] // CHUNKS
    particles = cloud.shape[0]
    block = min(256, people)
    steps = people // block
    with_gram = chunk == 0
    lanes = people // 2 + (LANES if with_gram else 0)
    exchanged = jax.ShapeDtypeStruct((particles, lanes), F32)
    return pl.pallas_call(
        functools.partial(center_kernel, block, with_gram),
        grid=(steps,),
        in_specs=[
            pl.BlockSpec((block, variants), lambda i: (chunk * steps + i, 0)),
            pl.BlockSpec((particles, variants), lambda i: (0, 0), pipeline_mode=pl.Buffered(1)),
            VMEM,
        ],
        out_specs=[VMEM, VMEM, VMEM],
        out_shape=[pltpu.VMEM((people, variants), BF16), exchanged, exchanged],
        scratch_shapes=[
            pltpu.VMEM((particles, variants), BF16),
            pltpu.VMEM((particles, people), F32),
            pltpu.VMEM((particles, LANES), F32),
        ],
        compiler_params=params(28),
        cost_estimate=cost(16 * particles * people * variants),
        name="center_and_first_logits",
    )(doses, cloud, scalars)


def residual_kernel(parts, people, chunks, scale, earlier, tail, gram, loglik_as, status, *refs):
    sent, refs = refs[:parts], list(refs[parts:])
    before = refs.pop(0) if earlier else None
    half = people // 2
    outcome = jnp.concatenate(
        [
            status[:, pl.ds(pl.multiple_of(chunk * people + core_of() * half, half), half)]
            for chunk in chunks
        ],
        axis=1,
    ).astype(F32)
    share = half * len(chunks)
    values = tree_sum([ref[...].astype(F32) for ref in sent])
    logits = values[:, :share] * scale
    residual = refs.pop(0)
    residual[:, :share] = (outcome - jax.nn.sigmoid(logits)).astype(BF16)
    if loglik_as or tail:
        softplus = jnp.maximum(logits, 0.0) + jnp.log1p(jnp.exp(-jnp.abs(logits)))
        loglik = jnp.sum(outcome * logits - softplus, axis=1, keepdims=True)
        if earlier:
            loglik = loglik + before[...]
        if tail:
            residual[:, share:] = as_lanes(loglik)
        if loglik_as:
            refs.pop(0)[...] = loglik if loglik_as == "column" else flipped(loglik)
    if gram:
        refs.pop(0)[...] = values[:, share:]


def residual_of(scale, status, chunks, sent, earlier=None, tail=False, gram=False, loglik_as=None):
    particles = sent[0].shape[0]
    people = status.shape[1] // CHUNKS
    share = people // 2 * len(chunks)
    out_shape = [jax.ShapeDtypeStruct((particles, share + (LANES if tail else 0)), BF16)]
    if loglik_as:
        shape = (particles, 1) if loglik_as == "column" else (1, particles)
        out_shape.append(jax.ShapeDtypeStruct(shape, F32))
    if gram:
        out_shape.append(jax.ShapeDtypeStruct((particles, LANES), F32))
    operands = [status, *sent] + ([earlier] if earlier is not None else [])
    return pl.pallas_call(
        functools.partial(
            residual_kernel, len(sent), people, chunks, scale, earlier is not None, tail, gram, loglik_as
        ),
        in_specs=[VMEM] * len(operands),
        out_specs=[VMEM] * len(out_shape),
        out_shape=out_shape,
        compiler_params=params(12),
        name="residual",
    )(*operands)


def gradient_kernel(count, which, piece, tail, *refs):
    pairs, centered = refs[: 2 * count], refs[2 * count : 2 * count + CHUNKS]
    grad, residual = refs[2 * count + CHUNKS :]
    people, variants = centered[0].shape
    half = people // 2
    mine = core_of()
    for chunk in range(CHUNKS):
        own, other = (pairs[2 * chunk], pairs[2 * chunk + 1]) if count == CHUNKS else pairs
        at = 0 if count == CHUNKS else chunk * half
        base = chunk * people
        residual[:, pl.ds(pl.multiple_of(base + mine * half, half), half)] = own[:, at : at + half]
        residual[:, pl.ds(pl.multiple_of(base + (1 - mine) * half, half), half)] = other[
            :, at : at + half
        ]
    columns = variants // 2 // PIECES
    width = tile_of(columns, 512)
    first = half_of(which, piece, variants)
    for start in range(0, columns, width):
        grad[:, start : start + width] = sum(
            jnp.dot(
                residual[:, chunk * people : (chunk + 1) * people],
                centered[chunk][:, pl.ds(pl.multiple_of(first + start, width), width)],
                preferred_element_type=F32,
            )
            for chunk in range(CHUNKS)
        ).astype(BF16)
    if tail:
        grad[:, columns:] = as_lanes(from_lanes(own[:, half:]) + from_lanes(other[:, half:]))


def gradient(which, piece, pairs, centered, tail):
    particles = pairs[0].shape[0]
    people = sum(c.shape[0] for c in centered)
    columns = centered[0].shape[1] // 2 // PIECES
    return pl.pallas_call(
        functools.partial(gradient_kernel, len(pairs) // 2, which, piece, tail),
        in_specs=[VMEM] * (len(pairs) + CHUNKS),
        out_specs=VMEM,
        out_shape=jax.ShapeDtypeStruct((particles, columns + (LANES if tail else 0)), BF16),
        scratch_shapes=[pltpu.VMEM((particles, people), BF16)],
        compiler_params=params(8),
        cost_estimate=cost(8 * particles * people * columns),
        name="gradient",
    )(*pairs, *centered)


def pair_sum_kernel(columns, tail, left, right, out):
    total = left[:, :columns].astype(F32) + right[:, :columns].astype(F32)
    out[:, :columns] = total.astype(BF16)
    if tail:
        out[:, columns:] = as_lanes(from_lanes(left[:, columns:]) + from_lanes(right[:, columns:]))


def pair_sum(columns, tail, left, right):
    return pl.pallas_call(
        functools.partial(pair_sum_kernel, columns, tail),
        in_specs=[VMEM, VMEM],
        out_specs=VMEM,
        out_shape=jax.ShapeDtypeStruct((left.shape[0], columns + (LANES if tail else 0)), BF16),
        compiler_params=params(8),
        name="pair_sum",
    )(left, right)


def weigh(total_variants, heat_advance, loglik, gram):
    scaled = heat_advance * loglik
    clipped = jnp.maximum(scaled - jnp.max(scaled, axis=0, keepdims=True), -CLIP_FLOOR)
    log_weights = clipped - jnp.log(jnp.sum(jnp.exp(clipped), axis=0, keepdims=True))
    weights = jnp.exp(log_weights)
    particles = loglik.shape[0]
    gram = gram[:, :particles]
    diagonal = lax.broadcasted_iota(jnp.int32, gram.shape, 0) == lax.broadcasted_iota(
        jnp.int32, gram.shape, 1
    )
    square = jnp.sum(jnp.where(diagonal, gram * weights, 0.0), axis=0, keepdims=True)
    mixed = jnp.sum(weights * gram, axis=0, keepdims=True) * flipped(weights)
    total = jnp.sum(square - mixed, axis=1, keepdims=True)
    return log_weights, weights, total / total_variants + 1e-06


def update_kernel(which, move, total_variants, scalars, flags, noise, *refs):
    refs = list(refs)
    centered = [refs.pop(0) for _ in range(CHUNKS)]
    grads = [refs.pop(0) for _ in range(PIECES)]
    cloud = refs.pop(0)
    start_first, last = move == 0, move == 1
    people, variants = centered[0].shape
    columns = variants // 2
    advance = scalars[:, 1:2]
    heat = (scalars[:, 0:1] + advance) * float(total_variants) ** (-0.5)
    approved = flipped(flags[move : move + 1, :].astype(F32)) > 0.5
    if start_first and which == KEEP:
        gram, arrived, held = refs.pop(0), refs.pop(0), refs.pop(0)
    elif start_first:
        weights, factor = refs.pop(0)[...], refs.pop(0)[...]
    else:
        size_in = refs.pop(0)
    before = refs.pop(0) if which == SEND else None
    if last and which == SEND:
        refs.pop(0)
    moved = refs.pop(0)
    if start_first:
        size_out = refs.pop(0)
        if which == KEEP:
            log_weights_out, weights_out, factor_out = refs.pop(0), refs.pop(0), refs.pop(0)
            loglik = from_lanes(held[:, columns // PIECES :]) + from_lanes(arrived[:, columns // PIECES :])
            log_weights, weights, mean_spread = weigh(total_variants, advance, loglik, gram[...])
            log_weights_out[...] = flipped(log_weights)
            weights_out[...] = weights
            factor = scalars[:, 2:3] / mean_spread
            factor_out[...] = factor
    if which == KEEP:
        total = refs.pop(0)
    else:
        mine, other, total = refs.pop(0), refs.pop(0), refs.pop(0)
    if last:
        buffer, sems = refs
    copies = []
    width = tile_of(columns // PIECES, 2048)
    narrow = tile_of(width, 512)
    at_block = []
    for piece in range(PIECES):
        first = half_of(which, piece, variants)
        at_block += [first + start for start in range(0, columns // PIECES, width)]
    for block, first in enumerate(at_block):
        chosen = []
        for start in range(block * width, (block + 1) * width, narrow):
            there = pl.ds(pl.multiple_of(first + start - block * width, narrow), narrow)
            here = slice(start, start + narrow)
            c = cloud[:, there] if start_first else cloud[:, here]
            if start_first:
                center = jnp.sum(weights * c, axis=0, keepdims=True)
                spread = jnp.sum(weights * (c - center) ** 2, axis=0, keepdims=True) + 1e-06
                size = spread * factor
                size_out[:, here] = size
            else:
                size = size_in[:, here]
            piece, at = divmod(start, columns // PIECES)
            slope = grads[piece][:, at : at + narrow].astype(F32)
            rise = heat * slope - SHRINKAGE_LEVEL * c * lax.rsqrt(c * c + 1.0)
            proposal = c + size * rise + jnp.sqrt(2.0 * size) * noise[move, :, there]
            c = jnp.where(approved, proposal, c)
            (buffer if last else moved)[:, here] = c
            chosen.append(c.astype(BF16))
        there = pl.ds(pl.multiple_of(first, width), width)
        if last:
            copies.append(
                pltpu.make_async_copy(
                    buffer.at[:, pl.ds(block * width, width)], moved.at[:, there], sems.at[block]
                )
            )
            copies[-1].start()
        chosen = jnp.concatenate(chosen, axis=1)
        for chunk in range(CHUNKS):
            rows = slice(chunk * people, (chunk + 1) * people)
            term = rows_dot(centered[chunk][:, there], chosen)
            if block > 0:
                term = total[rows, :] + term
            elif which == SEND:
                term = before[rows, :] + term
            total[rows, :] = term
    if which == SEND:
        half = people // 2
        here = core_of()
        for chunk in range(CHUNKS):
            out = slice(chunk * half, (chunk + 1) * half)
            base = chunk * people
            mine[:, out] = total[pl.ds(pl.multiple_of(base + here * half, half), half), :].T
            other[:, out] = total[pl.ds(pl.multiple_of(base + (1 - here) * half, half), half), :].T
    for copy in copies:
        copy.wait()


def update(which, move, total_variants, fixed, centered, grads, cloud, extra, before, moved):
    flags = fixed[1]
    particles, variants = flags.shape[1], centered[0].shape[1]
    people = sum(c.shape[0] for c in centered)
    columns = variants // 2
    operands = [*fixed, *centered, *grads, cloud, *extra]
    if before is not None:
        operands.append(before)
    aliases = {}
    if moved is not None:
        aliases = {len(operands): 0}
        operands.append(moved)
    last = move == 1
    out_shape = [jax.ShapeDtypeStruct((particles, variants if last else columns), F32)]
    if not last:
        out_shape.append(jax.ShapeDtypeStruct((1, columns), F32))
        if which == KEEP:
            out_shape.append(jax.ShapeDtypeStruct((1, particles), F32))
            out_shape.append(jax.ShapeDtypeStruct((particles, 1), F32))
            out_shape.append(jax.ShapeDtypeStruct((1, 1), F32))
    scratch = []
    if which == KEEP:
        out_shape.append(jax.ShapeDtypeStruct((people, particles), F32))
    else:
        out_shape += [jax.ShapeDtypeStruct((particles, people // 2), F32)] * 2
        scratch.append(pltpu.VMEM((people, particles), F32))
    if last:
        blocks = columns // tile_of(columns // PIECES, 2048)
        scratch += [pltpu.VMEM((particles, columns), F32), pltpu.SemaphoreType.DMA((blocks,))]
    specs = [VMEM] * len(operands)
    if moved is not None:
        specs[-1] = HBM
    return pl.pallas_call(
        functools.partial(update_kernel, which, move, total_variants),
        in_specs=specs,
        out_specs=[HBM if last else VMEM] + [VMEM] * (len(out_shape) - 1),
        out_shape=out_shape,
        input_output_aliases=aliases,
        scratch_shapes=scratch,
        compiler_params=params(12),
        cost_estimate=cost(8 * particles * people * columns),
        name="update_and_logits",
    )(*operands)


def swap(value, axis, distance):
    size = lax.axis_size(axis)
    return lax.ppermute(value, axis, [(i, i ^ distance) for i in range(size)])


def tree_sum(values):
    values = list(values)
    while len(values) > 1:
        values = [values[i] + values[i + 1] for i in range(0, len(values), 2)]
    return values[0]


def swap_over_rows(value, piece, stage):
    rows, columns = lax.axis_size("row"), lax.axis_size("col")
    bits = row_bits()
    order = (bits[stage], bits[::-1][stage])
    return lax.ppermute(
        value,
        ("row", "col"),
        [
            (row * columns + col, (row ^ order[piece % 2]) * columns + col)
            for row in range(rows)
            for col in range(columns)
        ],
    )


def over_chips(mine, other, link):
    mine = (mine + swap(other, "col", 1)).astype(link)
    return [mine] + [swap(mine, "col", d) for d in range(2, lax.axis_size("col"), 2)]


def over_chips_by_stages(mine, other):
    mine = mine + swap(other, "col", 1)
    size = lax.axis_size("col")
    bits = [1 << b for b in range(1, size.bit_length() - 1)]
    for stage, order in enumerate(zip(bits, bits[::-1])):
        arrived = lax.ppermute(mine, "col", [(i, i ^ order[i % 2]) for i in range(size)])
        if stage < len(bits) - 1:
            mine = mine + arrived
    return [mine, arrived]


def sum_small(value):
    value = value + swap(value, "col", 1)
    size = lax.axis_size("row")
    return tree_sum([value] + [swap(value, "row", d) for d in range(1, size)])


def local(
    allele_doses,
    disease_status,
    walker_cloud,
    normal_perturbations,
    approval_flags,
    present_heat,
    heat_advance,
    drift_magnitude,
):
    people, variants = allele_doses.shape
    total_variants = variants * lax.axis_size("col")
    total_people = people * lax.axis_size("row")
    scale = float(total_variants) ** (-0.5)
    status = disease_status.reshape(1, people)
    scalars = jnp.concatenate([present_heat, heat_advance, drift_magnitude])[None, :]

    centered, pairs, loglik, gram, sent = [], [], None, None, None
    for chunk in range(CHUNKS + 1):
        if chunk < CHUNKS:
            part, mine, other = center_and_first_logits(chunk, allele_doses, walker_cloud, scalars)
            centered.append(part)
        if chunk > 0:
            if chunk < CHUNKS:
                (mine, other), sent = lax.optimization_barrier(((mine, other), sent))
            tail = chunk == CHUNKS
            own, *extra = residual_of(
                scale,
                status,
                (chunk - 1,),
                sent,
                earlier=loglik,
                tail=tail,
                gram=chunk == 1,
                loglik_as=None if tail else "column",
            )
            if chunk == 1:
                gram = extra.pop()
            if not tail:
                (loglik,) = extra
            pairs += [own, swap(own, "col", 1)]
        if chunk < CHUNKS:
            sent = over_chips_by_stages(mine, other)

    width = variants // 2 // PIECES
    fixed = (scalars, approval_flags, normal_perturbations)
    stages = len(row_bits())
    pieces = range(PIECES)
    for move in range(2):
        first = move == 0
        tails = [first and piece == 0 for piece in pieces]
        arrived = [
            swap_over_rows(gradient(SEND, piece, pairs, centered, tails[piece]), piece, 0)
            for piece in pieces
        ]
        held = [gradient(KEEP, piece, pairs, centered, tails[piece]) for piece in pieces]
        for stage in range(1, stages):
            held = [pair_sum(width, *each) for each in zip(tails, held, arrived)]
            arrived = [swap_over_rows(each, piece, stage) for piece, each in enumerate(held)]
        summed = [pair_sum(width, False, *each) for each in zip(held, arrived)]
        arriving = [swap_over_rows(each, piece, 0) for piece, each in enumerate(summed)]
        if first:
            c_kept, size_kept, log_weights, weights, factor, total = update(
                KEEP, move, total_variants, fixed, centered, summed, walker_cloud,
                [gram, arrived[0], held[0]], None, None,
            )
            c_sent, size_sent, mine, other = update(
                SEND, move, total_variants, fixed, centered, arriving, walker_cloud,
                [weights, factor], total, None,
            )
        else:
            moved, total = update(
                KEEP, move, total_variants, fixed, centered, summed, c_kept, [size_kept], None, None
            )
            moved, mine, other = update(
                SEND, move, total_variants, fixed, centered, arriving, c_sent, [size_sent], total, moved
            )
        sent = over_chips(mine, other, BF16)
        if first:
            (own,) = residual_of(scale, status, tuple(range(CHUNKS)), sent)
            pairs = [own, swap(own, "col", 1)]
        else:
            _, loglik = residual_of(
                scale, status, tuple(range(CHUNKS)), sent, loglik_as="row"
            )
    mean_loglik = sum_small(loglik) / total_people
    return (moved, log_weights[0], mean_loglik[0])


def solution(mesh):
    placed = (P("row", "col"), P("row"), P(None, "col"), P(None, None, "col"), P(), P(), P(), P())
    return jax.shard_map(
        local, mesh=mesh, in_specs=placed, out_specs=(P(None, "col"), P(), P()), check_vma=False
    )
```

```python
import functools

import jax
import jax.numpy as jnp
from jax import lax
from jax.experimental import pallas as pl
from jax.experimental.pallas import tpu as pltpu
from jax.sharding import PartitionSpec as P

CLIP_FLOOR = 4.0
SHRINKAGE_LEVEL = 0.5
F32 = jnp.float32
BF16 = jnp.bfloat16
VMEM = pl.BlockSpec(memory_space=pltpu.VMEM)
SMEM = pl.BlockSpec(memory_space=pltpu.SMEM)
HBM = pl.BlockSpec(memory_space=pltpu.HBM)
KEEP, SEND = 0, 1
MIB = 1 << 20
LANES = 128
CHUNKS = 1
PIECES = 4


def core_of():
    return lax.rem(lax.axis_index("col"), 2)


def row_bits():
    return [1 << b for b in range(lax.axis_size("row").bit_length() - 1)]


def half_of(which, piece, variants):
    columns = variants // PIECES
    bits = row_bits()
    bit = jnp.where(lax.rem(jnp.int32(piece), 2) == 0, bits[0], bits[-1])
    own = lax.rem(lax.div(lax.axis_index("row"), bit), 2)
    chosen = own if which == KEEP else 1 - own
    return pl.multiple_of(piece * columns + chosen * (columns // 2), columns // 2)


def rows_dot(left, right):
    return lax.dot_general(left, right, (((1,), (1,)), ((), ())), preferred_element_type=F32)


def tile_of(size, most):
    while size % most:
        most //= 2
    return most


def params(mib):
    return pltpu.CompilerParams(vmem_limit_bytes=mib * MIB)


def cost(flops):
    return pl.CostEstimate(flops=flops, bytes_accessed=0, transcendentals=0)


def as_lanes(value):
    high = value.astype(BF16)
    rest = value - high.astype(F32)
    middle = rest.astype(BF16)
    low = (rest - middle.astype(F32)).astype(BF16)
    lane = lax.broadcasted_iota(jnp.int32, (value.shape[0], LANES), 1)
    zero = jnp.zeros((value.shape[0], LANES), F32)
    out = jnp.where(lane == 0, high.astype(F32), zero)
    out = jnp.where(lane == 1, middle.astype(F32), out)
    return jnp.where(lane == 2, low.astype(F32), out).astype(BF16)


def flipped(value):
    size = max(value.shape)
    diagonal = lax.broadcasted_iota(jnp.int32, (size, size), 0) == lax.broadcasted_iota(
        jnp.int32, (size, size), 1
    )
    return jnp.sum(
        jnp.where(diagonal, value, 0.0), axis=int(value.shape[0] == 1), keepdims=True
    )


def from_lanes(lanes):
    return jnp.sum(lanes.astype(F32), axis=1, keepdims=True)


def center_kernel(block, with_gram, doses, cloud, _, centered, mine, other, cloud_bf, logits, gram):
    step = pl.program_id(0)
    variants = doses.shape[1]
    people = logits.shape[1]
    half = people // 2

    @pl.when(step == 0)
    def _():
        cloud_bf[...] = cloud[...].astype(BF16)

    if with_gram:

        @pl.when(step == 0)
        def _():
            width = tile_of(variants, 1024)
            total = None
            for start in range(0, variants, width):
                c = cloud[:, start : start + width]
                c = c - jnp.mean(c, axis=0, keepdims=True)
                high = c.astype(BF16)
                low = (c - high.astype(F32)).astype(BF16)
                term = rows_dot(high, high) + 2.0 * rows_dot(high, low)
                total = term if total is None else total + term
            gram[...] = jnp.zeros(gram.shape, F32)
            gram[:, : total.shape[1]] = total

    width = tile_of(variants, 2048)
    total = None
    for start in range(0, variants, width):
        part = (doses[:, start : start + width] - 1).astype(F32).astype(BF16)
        centered[pl.ds(pl.multiple_of(step * block, block), block), start : start + width] = part
        term = rows_dot(part, cloud_bf[:, start : start + width])
        total = term if total is None else total + term
    logits[:, pl.ds(pl.multiple_of(step * block, block), block)] = total.T

    @pl.when(step == pl.num_programs(0) - 1)
    def _():
        first = core_of()
        mine[:, :half] = logits[:, pl.ds(pl.multiple_of(first * half, half), half)]
        other[:, :half] = logits[:, pl.ds(pl.multiple_of((1 - first) * half, half), half)]
        if with_gram:
            mine[:, half:] = gram[...]
            other[:, half:] = gram[...]


def center_and_first_logits(chunk, doses, cloud, scalars):
    variants = doses.shape[1]
    people = doses.shape[0] // CHUNKS
    particles = cloud.shape[0]
    block = min(256, people)
    steps = people // block
    with_gram = chunk == 0
    lanes = people // 2 + (LANES if with_gram else 0)
    exchanged = jax.ShapeDtypeStruct((particles, lanes), F32)
    return pl.pallas_call(
        functools.partial(center_kernel, block, with_gram),
        grid=(steps,),
        in_specs=[
            pl.BlockSpec((block, variants), lambda i: (chunk * steps + i, 0)),
            pl.BlockSpec((particles, variants), lambda i: (0, 0), pipeline_mode=pl.Buffered(1)),
            VMEM,
        ],
        out_specs=[VMEM, VMEM, VMEM],
        out_shape=[pltpu.VMEM((people, variants), BF16), exchanged, exchanged],
        scratch_shapes=[
            pltpu.VMEM((particles, variants), BF16),
            pltpu.VMEM((particles, people), F32),
            pltpu.VMEM((particles, LANES), F32),
        ],
        compiler_params=params(28),
        cost_estimate=cost(16 * particles * people * variants),
        name="center_and_first_logits",
    )(doses, cloud, scalars)


def residual_kernel(scale, tail, status, *refs):
    sent, out = refs[:-1], refs[-1]
    people = sent[0].shape[1]
    outcome = outcome_of(status)
    logits = tree_sum([ref[...].astype(F32) for ref in sent]) * scale
    out[:, :people] = (outcome - jax.nn.sigmoid(logits)).astype(BF16)
    if tail:
        out[:, people:] = as_lanes(loglik_of(outcome, logits))


def residual_of(scale, status, sent, tail=False):
    particles, people = sent[0].shape
    return pl.pallas_call(
        functools.partial(residual_kernel, scale, tail),
        in_specs=[VMEM] * (1 + len(sent)),
        out_specs=VMEM,
        out_shape=jax.ShapeDtypeStruct((particles, people + (LANES if tail else 0)), BF16),
        compiler_params=params(8),
        name="residual",
    )(status, *sent)


def outcome_of(status):
    half = status.shape[1] // 2
    return status[:, pl.ds(pl.multiple_of(core_of() * half, half), half)].astype(F32)


def loglik_of(outcome, logits):
    softplus = jnp.maximum(logits, 0.0) + jnp.log1p(jnp.exp(-jnp.abs(logits)))
    return jnp.sum(outcome * logits - softplus, axis=1, keepdims=True)


def last_loglik_kernel(scale, status, *refs):
    logits = tree_sum([ref[...].astype(F32) for ref in refs[:-1]]) * scale
    refs[-1][...] = flipped(loglik_of(outcome_of(status), logits))


def last_loglik(scale, status, sent):
    return pl.pallas_call(
        functools.partial(last_loglik_kernel, scale),
        in_specs=[VMEM] * (1 + len(sent)),
        out_specs=VMEM,
        out_shape=jax.ShapeDtypeStruct((1, sent[0].shape[0]), F32),
        compiler_params=params(8),
        name="last_loglik",
    )(status, *sent)


def gradient_kernel(count, which, piece, tail, *refs):
    pairs, centered = refs[: 2 * count], refs[2 * count : 2 * count + CHUNKS]
    grad, residual = refs[2 * count + CHUNKS :]
    people, variants = centered[0].shape
    half = people // 2
    mine = core_of()
    for chunk in range(CHUNKS):
        own, other = (pairs[2 * chunk], pairs[2 * chunk + 1]) if count == CHUNKS else pairs
        at = 0 if count == CHUNKS else chunk * half
        base = chunk * people
        residual[:, pl.ds(pl.multiple_of(base + mine * half, half), half)] = own[:, at : at + half]
        residual[:, pl.ds(pl.multiple_of(base + (1 - mine) * half, half), half)] = other[
            :, at : at + half
        ]
    columns = variants // 2 // PIECES
    width = tile_of(columns, 512)
    first = half_of(which, piece, variants)
    for start in range(0, columns, width):
        grad[:, start : start + width] = sum(
            jnp.dot(
                residual[:, chunk * people : (chunk + 1) * people],
                centered[chunk][:, pl.ds(pl.multiple_of(first + start, width), width)],
                preferred_element_type=F32,
            )
            for chunk in range(CHUNKS)
        ).astype(BF16)
    if tail:
        grad[:, columns:] = as_lanes(from_lanes(own[:, half:]) + from_lanes(other[:, half:]))


def gradient(which, piece, pairs, centered, tail):
    particles = pairs[0].shape[0]
    people = sum(c.shape[0] for c in centered)
    columns = centered[0].shape[1] // 2 // PIECES
    return pl.pallas_call(
        functools.partial(gradient_kernel, len(pairs) // 2, which, piece, tail),
        in_specs=[VMEM] * (len(pairs) + CHUNKS),
        out_specs=VMEM,
        out_shape=jax.ShapeDtypeStruct((particles, columns + (LANES if tail else 0)), BF16),
        scratch_shapes=[pltpu.VMEM((particles, people), BF16)],
        compiler_params=params(8),
        cost_estimate=cost(8 * particles * people * columns),
        name="gradient",
    )(*pairs, *centered)


def pair_sum_kernel(columns, tail, left, right, out):
    total = left[:, :columns].astype(F32) + right[:, :columns].astype(F32)
    out[:, :columns] = total.astype(BF16)
    if tail:
        out[:, columns:] = as_lanes(from_lanes(left[:, columns:]) + from_lanes(right[:, columns:]))


def pair_sum(columns, tail, left, right):
    return pl.pallas_call(
        functools.partial(pair_sum_kernel, columns, tail),
        in_specs=[VMEM, VMEM],
        out_specs=VMEM,
        out_shape=jax.ShapeDtypeStruct((left.shape[0], columns + (LANES if tail else 0)), BF16),
        compiler_params=params(8),
        name="pair_sum",
    )(left, right)


def weigh(total_variants, heat_advance, loglik, gram):
    scaled = heat_advance * loglik
    clipped = jnp.maximum(scaled - jnp.max(scaled, axis=0, keepdims=True), -CLIP_FLOOR)
    log_weights = clipped - jnp.log(jnp.sum(jnp.exp(clipped), axis=0, keepdims=True))
    weights = jnp.exp(log_weights)
    particles = loglik.shape[0]
    gram = gram[:, :particles]
    diagonal = lax.broadcasted_iota(jnp.int32, gram.shape, 0) == lax.broadcasted_iota(
        jnp.int32, gram.shape, 1
    )
    square = jnp.sum(jnp.where(diagonal, gram * weights, 0.0), axis=0, keepdims=True)
    mixed = jnp.sum(weights * gram, axis=0, keepdims=True) * flipped(weights)
    total = jnp.sum(square - mixed, axis=1, keepdims=True)
    return log_weights, weights, total / total_variants + 1e-06


def update_kernel(which, move, total_variants, chips, scalars, flags, noise, *refs):
    refs = list(refs)
    centered = [refs.pop(0) for _ in range(CHUNKS)]
    grads = [refs.pop(0) for _ in range(PIECES)]
    cloud = refs.pop(0)
    start_first, last = move == 0, move == 1
    people, variants = centered[0].shape
    columns = variants // 2
    advance = scalars[:, 1:2]
    heat = (scalars[:, 0:1] + advance) * float(total_variants) ** (-0.5)
    approved = flipped(flags[move : move + 1, :].astype(F32)) > 0.5
    if start_first and which == KEEP:
        gram = tree_sum([refs.pop(0)[...] for _ in range(chips)])
        arrived, held = refs.pop(0), refs.pop(0)
    elif start_first:
        weights, factor = refs.pop(0)[...], refs.pop(0)[...]
    else:
        size_in = refs.pop(0)
    before = refs.pop(0) if which == SEND else None
    if last and which == SEND:
        refs.pop(0)
    moved = refs.pop(0)
    if start_first:
        size_out = refs.pop(0)
        if which == KEEP:
            log_weights_out, weights_out, factor_out = refs.pop(0), refs.pop(0), refs.pop(0)
            loglik = from_lanes(held[:, columns // PIECES :]) + from_lanes(arrived[:, columns // PIECES :])
            log_weights, weights, mean_spread = weigh(total_variants, advance, loglik, gram)
            log_weights_out[...] = flipped(log_weights)
            weights_out[...] = weights
            factor = scalars[:, 2:3] / mean_spread
            factor_out[...] = factor
    if which == KEEP:
        total = refs.pop(0)
    else:
        mine, other, total = refs.pop(0), refs.pop(0), refs.pop(0)
    if last:
        buffer, sems = refs
    copies = []
    width = tile_of(columns // PIECES, 2048)
    narrow = tile_of(width, 512)
    at_block = []
    for piece in range(PIECES):
        first = half_of(which, piece, variants)
        at_block += [first + start for start in range(0, columns // PIECES, width)]
    for block, first in enumerate(at_block):
        chosen = []
        for start in range(block * width, (block + 1) * width, narrow):
            there = pl.ds(pl.multiple_of(first + start - block * width, narrow), narrow)
            here = slice(start, start + narrow)
            c = cloud[:, there] if start_first else cloud[:, here]
            if start_first:
                center = jnp.sum(weights * c, axis=0, keepdims=True)
                spread = jnp.sum(weights * (c - center) ** 2, axis=0, keepdims=True) + 1e-06
                size = spread * factor
                size_out[:, here] = size
            else:
                size = size_in[:, here]
            piece, at = divmod(start, columns // PIECES)
            slope = grads[piece][:, at : at + narrow].astype(F32)
            rise = heat * slope - SHRINKAGE_LEVEL * c * lax.rsqrt(c * c + 1.0)
            proposal = c + size * rise + jnp.sqrt(2.0 * size) * noise[move, :, there]
            c = jnp.where(approved, proposal, c)
            (buffer if last else moved)[:, here] = c
            chosen.append(c.astype(BF16))
        there = pl.ds(pl.multiple_of(first, width), width)
        if last:
            copies.append(
                pltpu.make_async_copy(
                    buffer.at[:, pl.ds(block * width, width)], moved.at[:, there], sems.at[block]
                )
            )
            copies[-1].start()
        chosen = jnp.concatenate(chosen, axis=1)
        for chunk in range(CHUNKS):
            rows = slice(chunk * people, (chunk + 1) * people)
            term = rows_dot(centered[chunk][:, there], chosen)
            if block > 0:
                term = total[rows, :] + term
            elif which == SEND:
                term = before[rows, :] + term
            total[rows, :] = term
    if which == SEND:
        half = people // 2
        here = core_of()
        for chunk in range(CHUNKS):
            out = slice(chunk * half, (chunk + 1) * half)
            base = chunk * people
            mine[:, out] = total[pl.ds(pl.multiple_of(base + here * half, half), half), :].T
            other[:, out] = total[pl.ds(pl.multiple_of(base + (1 - here) * half, half), half), :].T
    for copy in copies:
        copy.wait()


def update(which, move, total_variants, fixed, centered, grads, cloud, extra, before, moved):
    flags = fixed[1]
    particles, variants = flags.shape[1], centered[0].shape[1]
    people = sum(c.shape[0] for c in centered)
    columns = variants // 2
    operands = [*fixed, *centered, *grads, cloud, *extra]
    if before is not None:
        operands.append(before)
    aliases = {}
    if moved is not None:
        aliases = {len(operands): 0}
        operands.append(moved)
    last = move == 1
    out_shape = [jax.ShapeDtypeStruct((particles, variants if last else columns), F32)]
    if not last:
        out_shape.append(jax.ShapeDtypeStruct((1, columns), F32))
        if which == KEEP:
            out_shape.append(jax.ShapeDtypeStruct((1, particles), F32))
            out_shape.append(jax.ShapeDtypeStruct((particles, 1), F32))
            out_shape.append(jax.ShapeDtypeStruct((1, 1), F32))
    scratch = []
    if which == KEEP:
        out_shape.append(jax.ShapeDtypeStruct((people, particles), F32))
    else:
        out_shape += [jax.ShapeDtypeStruct((particles, people // 2), F32)] * 2
        scratch.append(pltpu.VMEM((people, particles), F32))
    if last:
        blocks = columns // tile_of(columns // PIECES, 2048)
        scratch += [pltpu.VMEM((particles, columns), F32), pltpu.SemaphoreType.DMA((blocks,))]
    specs = [VMEM] * len(operands)
    if moved is not None:
        specs[-1] = HBM
    return pl.pallas_call(
        functools.partial(update_kernel, which, move, total_variants, lax.axis_size("col") // 2),
        in_specs=specs,
        out_specs=[HBM if last else VMEM] + [VMEM] * (len(out_shape) - 1),
        out_shape=out_shape,
        input_output_aliases=aliases,
        scratch_shapes=scratch,
        compiler_params=params(12),
        cost_estimate=cost(8 * particles * people * columns),
        name="update_and_logits",
    )(*operands)


def swap(value, axis, distance):
    size = lax.axis_size(axis)
    return lax.ppermute(value, axis, [(i, i ^ distance) for i in range(size)])


def tree_sum(values):
    values = list(values)
    while len(values) > 1:
        values = [values[i] + values[i + 1] for i in range(0, len(values), 2)]
    return values[0]


def swap_over_rows(value, piece, stage):
    rows, columns = lax.axis_size("row"), lax.axis_size("col")
    bits = row_bits()
    order = (bits[stage], bits[::-1][stage])
    return lax.ppermute(
        value,
        ("row", "col"),
        [
            (row * columns + col, (row ^ order[piece % 2]) * columns + col)
            for row in range(rows)
            for col in range(columns)
        ],
    )


def over_chips(mine):
    return [mine] + [swap(mine, "col", d) for d in range(2, lax.axis_size("col"), 2)]


def sum_small(value):
    value = value + swap(value, "col", 1)
    size = lax.axis_size("row")
    return tree_sum([value] + [swap(value, "row", d) for d in range(1, size)])


def local(
    allele_doses,
    disease_status,
    walker_cloud,
    normal_perturbations,
    approval_flags,
    present_heat,
    heat_advance,
    drift_magnitude,
):
    people, variants = allele_doses.shape
    total_variants = variants * lax.axis_size("col")
    total_people = people * lax.axis_size("row")
    scale = float(total_variants) ** (-0.5)
    status = disease_status.reshape(1, people)
    scalars = jnp.concatenate([present_heat, heat_advance, drift_magnitude])[None, :]

    part, mine, other = center_and_first_logits(0, allele_doses, walker_cloud, scalars)
    centered = [part]
    mine = mine + swap(other, "col", 1)
    sent = over_chips((mine[:, : people // 2] * scale).astype(jnp.float16))
    own = residual_of(1.0, status, [tree_sum([each.astype(F32) for each in sent])], tail=True)
    pairs = [own, swap(own, "col", 1)]
    gram = mine[:, people // 2 :]

    width = variants // 2 // PIECES
    fixed = (scalars, approval_flags, normal_perturbations)
    stages = len(row_bits())
    pieces = range(PIECES)
    for move in range(2):
        first = move == 0
        tails = [first and piece == 0 for piece in pieces]
        arrived = [
            swap_over_rows(gradient(SEND, piece, pairs, centered, tails[piece]), piece, 0)
            for piece in pieces
        ]
        held = [gradient(KEEP, piece, pairs, centered, tails[piece]) for piece in pieces]
        if first:
            gram, held = lax.optimization_barrier((gram, held))
            grams = over_chips(gram)
        for stage in range(1, stages):
            held = [pair_sum(width, *each) for each in zip(tails, held, arrived)]
            arrived = [swap_over_rows(each, piece, stage) for piece, each in enumerate(held)]
        summed = [pair_sum(width, False, *each) for each in zip(held, arrived)]
        arriving = [swap_over_rows(each, piece, 0) for piece, each in enumerate(summed)]
        if first:
            c_kept, size_kept, log_weights, weights, factor, total = update(
                KEEP, move, total_variants, fixed, centered, summed, walker_cloud,
                [*grams, arrived[0], held[0]], None, None,
            )
            c_sent, size_sent, mine, other = update(
                SEND, move, total_variants, fixed, centered, arriving, walker_cloud,
                [weights, factor], total, None,
            )
        else:
            moved, total = update(
                KEEP, move, total_variants, fixed, centered, summed, c_kept, [size_kept], None, None
            )
            moved, mine, other = update(
                SEND, move, total_variants, fixed, centered, arriving, c_sent, [size_sent], total, moved
            )
        sent = over_chips((mine + swap(other, "col", 1)).astype(BF16))
        if first:
            own = residual_of(scale, status, sent)
            pairs = [own, swap(own, "col", 1)]
    loglik = last_loglik(scale, status, sent)
    mean_loglik = sum_small(loglik) / total_people
    return (moved, log_weights[0], mean_loglik[0])


def solution(mesh):
    placed = (P("row", "col"), P("row"), P(None, "col"), P(None, None, "col"), P(), P(), P(), P())
    return jax.shard_map(
        local, mesh=mesh, in_specs=placed, out_specs=(P(None, "col"), P(), P()), check_vma=False
    )
```

```python
import functools

import jax
import jax.numpy as jnp
from jax import lax
from jax.experimental import pallas as pl
from jax.experimental.pallas import tpu as pltpu
from jax.sharding import PartitionSpec as P

CLIP_FLOOR = 4.0
SHRINKAGE_LEVEL = 0.5
F32 = jnp.float32
BF16 = jnp.bfloat16
VMEM = pl.BlockSpec(memory_space=pltpu.VMEM)
SMEM = pl.BlockSpec(memory_space=pltpu.SMEM)
HBM = pl.BlockSpec(memory_space=pltpu.HBM)
KEEP, SEND = 0, 1
MIB = 1 << 20
LANES = 128
LOW_FACTOR = 2048.0
CHUNKS = 1
PIECES = 4


def core_of():
    return lax.rem(lax.axis_index("col"), 2)


def row_bits():
    return [1 << b for b in range(lax.axis_size("row").bit_length() - 1)]


def half_of(which, piece, variants):
    columns = variants // PIECES
    bits = row_bits()
    bit = jnp.where(lax.rem(jnp.int32(piece), 2) == 0, bits[0], bits[-1])
    own = lax.rem(lax.div(lax.axis_index("row"), bit), 2)
    chosen = own if which == KEEP else 1 - own
    return pl.multiple_of(piece * columns + chosen * (columns // 2), columns // 2)


def rows_dot(left, right):
    return lax.dot_general(left, right, (((1,), (1,)), ((), ())), preferred_element_type=F32)


def tile_of(size, most):
    while size % most:
        most //= 2
    return most


def params(mib):
    return pltpu.CompilerParams(vmem_limit_bytes=mib * MIB)


def cost(flops):
    return pl.CostEstimate(flops=flops, bytes_accessed=0, transcendentals=0)


def as_lanes(value):
    high = value.astype(BF16)
    rest = value - high.astype(F32)
    middle = rest.astype(BF16)
    low = (rest - middle.astype(F32)).astype(BF16)
    lane = lax.broadcasted_iota(jnp.int32, (value.shape[0], LANES), 1)
    zero = jnp.zeros((value.shape[0], LANES), F32)
    out = jnp.where(lane == 0, high.astype(F32), zero)
    out = jnp.where(lane == 1, middle.astype(F32), out)
    return jnp.where(lane == 2, low.astype(F32), out).astype(BF16)


def flipped(value):
    size = max(value.shape)
    diagonal = lax.broadcasted_iota(jnp.int32, (size, size), 0) == lax.broadcasted_iota(
        jnp.int32, (size, size), 1
    )
    return jnp.sum(
        jnp.where(diagonal, value, 0.0), axis=int(value.shape[0] == 1), keepdims=True
    )


def from_lanes(lanes):
    return jnp.sum(lanes.astype(F32), axis=1, keepdims=True)


def center_kernel(block, scale, total_variants, doses, cloud, _, centered, mine, other, cloud_bf, logits, gram):
    step = pl.program_id(0)
    variants = doses.shape[1]
    people = logits.shape[1]
    half = people // 2

    @pl.when(step == 0)
    def _():
        cloud_bf[...] = cloud[...].astype(BF16)

    @pl.when(step == 0)
    def _():
        width = tile_of(variants, 1024)
        total = None
        for start in range(0, variants, width):
            c = cloud[:, start : start + width]
            c = c - jnp.mean(c, axis=0, keepdims=True)
            high = c.astype(BF16)
            low = (c - high.astype(F32)).astype(BF16)
            term = rows_dot(high, high) + 2.0 * rows_dot(high, low)
            total = term if total is None else total + term
        gram[...] = total * (1.0 / total_variants)

    width = tile_of(variants, 2048)
    total = None
    for start in range(0, variants, width):
        part = (doses[:, start : start + width] - 1).astype(F32).astype(BF16)
        centered[pl.ds(pl.multiple_of(step * block, block), block), start : start + width] = part
        term = rows_dot(part, cloud_bf[:, start : start + width])
        total = term if total is None else total + term
    logits[:, pl.ds(pl.multiple_of(step * block, block), block)] = total.T

    @pl.when(step == pl.num_programs(0) - 1)
    def _():
        first = core_of()
        for which, out in ((first, mine), (1 - first, other)):
            out[:, :half] = logits[:, pl.ds(pl.multiple_of(which * half, half), half)] * scale
            out[:, half : half + LANES // 2] = gram[...]
            out[:, half + LANES // 2 :] = gram[...]


def center_and_first_logits(scale, total_variants, doses, cloud, scalars):
    variants = doses.shape[1]
    people = doses.shape[0]
    particles = cloud.shape[0]
    block = min(256, people)
    steps = people // block
    exchanged = jax.ShapeDtypeStruct((particles, people // 2 + LANES), F32)
    return pl.pallas_call(
        functools.partial(center_kernel, block, scale, total_variants),
        grid=(steps,),
        in_specs=[
            pl.BlockSpec((block, variants), lambda i: (i, 0)),
            pl.BlockSpec((particles, variants), lambda i: (0, 0), pipeline_mode=pl.Buffered(1)),
            VMEM,
        ],
        out_specs=[VMEM, VMEM, VMEM],
        out_shape=[pltpu.VMEM((people, variants), BF16), exchanged, exchanged],
        scratch_shapes=[
            pltpu.VMEM((particles, variants), BF16),
            pltpu.VMEM((particles, people), F32),
            pltpu.VMEM((particles, particles), F32),
        ],
        compiler_params=params(28),
        cost_estimate=cost(16 * particles * people * variants),
        name="center_and_first_logits",
    )(doses, cloud, scalars)


def first_residual_kernel(status, values, out, gram):
    people = status.shape[1] // 2
    particles = gram.shape[0]
    logits = values[:, :people]
    outcome = outcome_of(status)
    out[:, :people] = (outcome - jax.nn.sigmoid(logits)).astype(BF16)
    out[:, people:] = as_lanes(loglik_of(outcome, logits))
    middle = people + LANES // 2
    gram[...] = values[:, people : people + particles] + values[:, middle : middle + particles] * (
        1.0 / LOW_FACTOR
    )


def first_residual_of(status, values):
    particles = values.shape[0]
    return pl.pallas_call(
        first_residual_kernel,
        in_specs=[VMEM, VMEM],
        out_specs=[VMEM, VMEM],
        out_shape=[
            jax.ShapeDtypeStruct(values.shape, BF16),
            jax.ShapeDtypeStruct((particles, particles), F32),
        ],
        compiler_params=params(8),
        name="first_residual",
    )(status, values)


def residual_kernel(scale, status, *refs):
    logits = tree_sum([ref[...].astype(F32) for ref in refs[:-1]]) * scale
    refs[-1][...] = (outcome_of(status) - jax.nn.sigmoid(logits)).astype(BF16)


def residual_of(scale, status, sent):
    return pl.pallas_call(
        functools.partial(residual_kernel, scale),
        in_specs=[VMEM] * (1 + len(sent)),
        out_specs=VMEM,
        out_shape=jax.ShapeDtypeStruct(sent[0].shape, BF16),
        compiler_params=params(8),
        name="residual",
    )(status, *sent)


def outcome_of(status):
    half = status.shape[1] // 2
    return status[:, pl.ds(pl.multiple_of(core_of() * half, half), half)].astype(F32)


def loglik_of(outcome, logits):
    softplus = jnp.maximum(logits, 0.0) + jnp.log1p(jnp.exp(-jnp.abs(logits)))
    return jnp.sum(outcome * logits - softplus, axis=1, keepdims=True)


def last_loglik_kernel(scale, status, *refs):
    logits = tree_sum([ref[...].astype(F32) for ref in refs[:-1]]) * scale
    refs[-1][...] = flipped(loglik_of(outcome_of(status), logits))


def last_loglik(scale, status, sent):
    return pl.pallas_call(
        functools.partial(last_loglik_kernel, scale),
        in_specs=[VMEM] * (1 + len(sent)),
        out_specs=VMEM,
        out_shape=jax.ShapeDtypeStruct((1, sent[0].shape[0]), F32),
        compiler_params=params(8),
        name="last_loglik",
    )(status, *sent)


def gradient_kernel(count, which, piece, tail, *refs):
    pairs, centered = refs[: 2 * count], refs[2 * count : 2 * count + CHUNKS]
    grad, residual = refs[2 * count + CHUNKS :]
    people, variants = centered[0].shape
    half = people // 2
    mine = core_of()
    for chunk in range(CHUNKS):
        own, other = (pairs[2 * chunk], pairs[2 * chunk + 1]) if count == CHUNKS else pairs
        at = 0 if count == CHUNKS else chunk * half
        base = chunk * people
        residual[:, pl.ds(pl.multiple_of(base + mine * half, half), half)] = own[:, at : at + half]
        residual[:, pl.ds(pl.multiple_of(base + (1 - mine) * half, half), half)] = other[
            :, at : at + half
        ]
    columns = variants // 2 // PIECES
    width = tile_of(columns, 512)
    first = half_of(which, piece, variants)
    for start in range(0, columns, width):
        grad[:, start : start + width] = sum(
            jnp.dot(
                residual[:, chunk * people : (chunk + 1) * people],
                centered[chunk][:, pl.ds(pl.multiple_of(first + start, width), width)],
                preferred_element_type=F32,
            )
            for chunk in range(CHUNKS)
        ).astype(BF16)
    if tail:
        grad[:, columns:] = as_lanes(from_lanes(own[:, half:]) + from_lanes(other[:, half:]))


def gradient(which, piece, pairs, centered, tail):
    particles = pairs[0].shape[0]
    people = sum(c.shape[0] for c in centered)
    columns = centered[0].shape[1] // 2 // PIECES
    return pl.pallas_call(
        functools.partial(gradient_kernel, len(pairs) // 2, which, piece, tail),
        in_specs=[VMEM] * (len(pairs) + CHUNKS),
        out_specs=VMEM,
        out_shape=jax.ShapeDtypeStruct((particles, columns + (LANES if tail else 0)), BF16),
        scratch_shapes=[pltpu.VMEM((particles, people), BF16)],
        compiler_params=params(8),
        cost_estimate=cost(8 * particles * people * columns),
        name="gradient",
    )(*pairs, *centered)


def pair_sum_kernel(columns, tail, left, right, out):
    total = left[:, :columns].astype(F32) + right[:, :columns].astype(F32)
    out[:, :columns] = total.astype(BF16)
    if tail:
        out[:, columns:] = as_lanes(from_lanes(left[:, columns:]) + from_lanes(right[:, columns:]))


def pair_sum(columns, tail, left, right):
    return pl.pallas_call(
        functools.partial(pair_sum_kernel, columns, tail),
        in_specs=[VMEM, VMEM],
        out_specs=VMEM,
        out_shape=jax.ShapeDtypeStruct((left.shape[0], columns + (LANES if tail else 0)), BF16),
        compiler_params=params(8),
        name="pair_sum",
    )(left, right)


def weigh(heat_advance, loglik, gram):
    scaled = heat_advance * loglik
    clipped = jnp.maximum(scaled - jnp.max(scaled, axis=0, keepdims=True), -CLIP_FLOOR)
    log_weights = clipped - jnp.log(jnp.sum(jnp.exp(clipped), axis=0, keepdims=True))
    weights = jnp.exp(log_weights)
    particles = loglik.shape[0]
    gram = gram[:, :particles]
    diagonal = lax.broadcasted_iota(jnp.int32, gram.shape, 0) == lax.broadcasted_iota(
        jnp.int32, gram.shape, 1
    )
    square = jnp.sum(jnp.where(diagonal, gram * weights, 0.0), axis=0, keepdims=True)
    mixed = jnp.sum(weights * gram, axis=0, keepdims=True) * flipped(weights)
    total = jnp.sum(square - mixed, axis=1, keepdims=True)
    return log_weights, weights, total + 1e-06


def update_kernel(which, move, total_variants, scalars, flags, noise, *refs):
    refs = list(refs)
    centered = [refs.pop(0) for _ in range(CHUNKS)]
    grads = [refs.pop(0) for _ in range(PIECES)]
    cloud = refs.pop(0)
    start_first, last = move == 0, move == 1
    people, variants = centered[0].shape
    columns = variants // 2
    advance = scalars[:, 1:2]
    heat = (scalars[:, 0:1] + advance) * float(total_variants) ** (-0.5)
    approved = flipped(flags[move : move + 1, :].astype(F32)) > 0.5
    if start_first and which == KEEP:
        gram, arrived, held = refs.pop(0), refs.pop(0), refs.pop(0)
    elif start_first:
        weights, factor = refs.pop(0)[...], refs.pop(0)[...]
    else:
        size_in = refs.pop(0)
    before = refs.pop(0) if which == SEND else None
    if last and which == SEND:
        refs.pop(0)
    moved = refs.pop(0)
    if start_first:
        size_out = refs.pop(0)
        if which == KEEP:
            log_weights_out, weights_out, factor_out = refs.pop(0), refs.pop(0), refs.pop(0)
            loglik = from_lanes(held[:, columns // PIECES :]) + from_lanes(arrived[:, columns // PIECES :])
            log_weights, weights, mean_spread = weigh(advance, loglik, gram[...])
            log_weights_out[...] = flipped(log_weights)
            weights_out[...] = weights
            factor = scalars[:, 2:3] / mean_spread
            factor_out[...] = factor
    if which == KEEP:
        total = refs.pop(0)
    else:
        mine, other, total = refs.pop(0), refs.pop(0), refs.pop(0)
    if last:
        buffer, sems = refs
    copies = []
    width = tile_of(columns // PIECES, 2048)
    narrow = tile_of(width, 512)
    at_block = []
    for piece in range(PIECES):
        first = half_of(which, piece, variants)
        at_block += [first + start for start in range(0, columns // PIECES, width)]
    for block, first in enumerate(at_block):
        chosen = []
        for start in range(block * width, (block + 1) * width, narrow):
            there = pl.ds(pl.multiple_of(first + start - block * width, narrow), narrow)
            here = slice(start, start + narrow)
            c = cloud[:, there] if start_first else cloud[:, here]
            if start_first:
                center = jnp.sum(weights * c, axis=0, keepdims=True)
                spread = jnp.sum(weights * (c - center) ** 2, axis=0, keepdims=True) + 1e-06
                size = spread * factor
                size_out[:, here] = size
            else:
                size = size_in[:, here]
            piece, at = divmod(start, columns // PIECES)
            slope = grads[piece][:, at : at + narrow].astype(F32)
            rise = heat * slope - SHRINKAGE_LEVEL * c * lax.rsqrt(c * c + 1.0)
            proposal = c + size * rise + jnp.sqrt(2.0 * size) * noise[move, :, there]
            c = jnp.where(approved, proposal, c)
            (buffer if last else moved)[:, here] = c
            chosen.append(c.astype(BF16))
        there = pl.ds(pl.multiple_of(first, width), width)
        if last:
            copies.append(
                pltpu.make_async_copy(
                    buffer.at[:, pl.ds(block * width, width)], moved.at[:, there], sems.at[block]
                )
            )
            copies[-1].start()
        chosen = jnp.concatenate(chosen, axis=1)
        for chunk in range(CHUNKS):
            rows = slice(chunk * people, (chunk + 1) * people)
            term = rows_dot(centered[chunk][:, there], chosen)
            if block > 0:
                term = total[rows, :] + term
            elif which == SEND:
                term = before[rows, :] + term
            total[rows, :] = term
    if which == SEND:
        half = people // 2
        here = core_of()
        for chunk in range(CHUNKS):
            out = slice(chunk * half, (chunk + 1) * half)
            base = chunk * people
            mine[:, out] = total[pl.ds(pl.multiple_of(base + here * half, half), half), :].T
            other[:, out] = total[pl.ds(pl.multiple_of(base + (1 - here) * half, half), half), :].T
    for copy in copies:
        copy.wait()


def update(which, move, total_variants, fixed, centered, grads, cloud, extra, before, moved):
    flags = fixed[1]
    particles, variants = flags.shape[1], centered[0].shape[1]
    people = sum(c.shape[0] for c in centered)
    columns = variants // 2
    operands = [*fixed, *centered, *grads, cloud, *extra]
    if before is not None:
        operands.append(before)
    aliases = {}
    if moved is not None:
        aliases = {len(operands): 0}
        operands.append(moved)
    last = move == 1
    out_shape = [jax.ShapeDtypeStruct((particles, variants if last else columns), F32)]
    if not last:
        out_shape.append(jax.ShapeDtypeStruct((1, columns), F32))
        if which == KEEP:
            out_shape.append(jax.ShapeDtypeStruct((1, particles), F32))
            out_shape.append(jax.ShapeDtypeStruct((particles, 1), F32))
            out_shape.append(jax.ShapeDtypeStruct((1, 1), F32))
    scratch = []
    if which == KEEP:
        out_shape.append(jax.ShapeDtypeStruct((people, particles), F32))
    else:
        out_shape += [jax.ShapeDtypeStruct((particles, people // 2), F32)] * 2
        scratch.append(pltpu.VMEM((people, particles), F32))
    if last:
        blocks = columns // tile_of(columns // PIECES, 2048)
        scratch += [pltpu.VMEM((particles, columns), F32), pltpu.SemaphoreType.DMA((blocks,))]
    specs = [VMEM] * len(operands)
    if moved is not None:
        specs[-1] = HBM
    return pl.pallas_call(
        functools.partial(update_kernel, which, move, total_variants),
        in_specs=specs,
        out_specs=[HBM if last else VMEM] + [VMEM] * (len(out_shape) - 1),
        out_shape=out_shape,
        input_output_aliases=aliases,
        scratch_shapes=scratch,
        compiler_params=params(12),
        cost_estimate=cost(8 * particles * people * columns),
        name="update_and_logits",
    )(*operands)


def swap(value, axis, distance):
    size = lax.axis_size(axis)
    return lax.ppermute(value, axis, [(i, i ^ distance) for i in range(size)])


def tree_sum(values):
    values = list(values)
    while len(values) > 1:
        values = [values[i] + values[i + 1] for i in range(0, len(values), 2)]
    return values[0]


def after(value, earlier):
    return value if earlier is None else lax.optimization_barrier((value, earlier))[0]


def pair_sums(tails, held, arrived, width):
    sums = []
    for piece, tail in enumerate(tails):
        there = after(arrived[piece], sums[-1] if sums else None)
        sums.append(pair_sum(width, tail, held[piece], there))
    return sums


def swap_over_rows(value, piece, stage):
    rows, columns = lax.axis_size("row"), lax.axis_size("col")
    bits = row_bits()
    order = (bits[stage], bits[::-1][stage])
    return lax.ppermute(
        value,
        ("row", "col"),
        [
            (row * columns + col, (row ^ order[piece % 2]) * columns + col)
            for row in range(rows)
            for col in range(columns)
        ],
    )


def over_chips(mine):
    return [mine] + [swap(mine, "col", d) for d in range(2, lax.axis_size("col"), 2)]


def sum_small(value):
    value = value + swap(value, "col", 1)
    size = lax.axis_size("row")
    return tree_sum([value] + [swap(value, "row", d) for d in range(1, size)])


def local(
    allele_doses,
    disease_status,
    walker_cloud,
    normal_perturbations,
    approval_flags,
    present_heat,
    heat_advance,
    drift_magnitude,
):
    people, variants = allele_doses.shape
    total_variants = variants * lax.axis_size("col")
    total_people = people * lax.axis_size("row")
    scale = float(total_variants) ** (-0.5)
    status = disease_status.reshape(1, people)
    scalars = jnp.concatenate([present_heat, heat_advance, drift_magnitude])[None, :]

    part, mine, other = center_and_first_logits(
        scale, total_variants, allele_doses, walker_cloud, scalars
    )
    centered = [part]
    high, low = people // 2, people // 2 + LANES // 2
    values = mine + swap(other, "col", 1)
    lane = lax.broadcasted_iota(jnp.int32, values.shape, 1)
    rounded = lax.reduce_precision(values, exponent_bits=5, mantissa_bits=10)
    rest = (values - rounded) * LOW_FACTOR
    values = jnp.where(lane < high, values, jnp.where(lane < low, rounded, rest))
    sent = over_chips(values.astype(jnp.float16))
    own, gram = first_residual_of(status, tree_sum([each.astype(F32) for each in sent]))
    pairs = [own, swap(own, "col", 1)]

    width = variants // 2 // PIECES
    fixed = (scalars, approval_flags, normal_perturbations)
    stages = len(row_bits())
    pieces = range(PIECES)
    for move in range(2):
        first = move == 0
        tails = [first and piece == 0 for piece in pieces]
        sent_away = []
        for piece in pieces:
            there = after(pairs, sent_away[-1] if sent_away else None)
            sent_away.append(gradient(SEND, piece, there, centered, tails[piece]))
        arrived = [swap_over_rows(each, piece, 0) for piece, each in enumerate(sent_away)]
        for stage in range(1, stages):
            if stage == 1:
                held = []
                for piece in pieces:
                    there = after(pairs, held[piece - 2] if piece > 1 else sent_away[-1])
                    kept = gradient(KEEP, piece, there, centered, tails[piece])
                    there = after(arrived[piece], held[-1] if held else None)
                    held.append(pair_sum(width, tails[piece], kept, there))
            else:
                held = pair_sums(tails, held, arrived, width)
            arrived = [swap_over_rows(each, piece, stage) for piece, each in enumerate(held)]
        summed = pair_sums([False] * PIECES, held, arrived, width)
        arriving = [swap_over_rows(each, piece, 0) for piece, each in enumerate(summed)]
        if first:
            c_kept, size_kept, log_weights, weights, factor, total = update(
                KEEP, move, total_variants, fixed, centered, summed, walker_cloud,
                [gram, arrived[0], held[0]], None, None,
            )
            c_sent, size_sent, mine, other = update(
                SEND, move, total_variants, fixed, centered, arriving, walker_cloud,
                [weights, factor], total, None,
            )
        else:
            moved, total = update(
                KEEP, move, total_variants, fixed, centered, summed, c_kept, [size_kept], None, None
            )
            moved, mine, other = update(
                SEND, move, total_variants, fixed, centered, arriving, c_sent, [size_sent], total, moved
            )
        sent = over_chips((mine + swap(other, "col", 1)).astype(BF16))
        if first:
            own = residual_of(scale, status, sent)
            pairs = [own, swap(own, "col", 1)]
    loglik = last_loglik(scale, status, sent)
    mean_loglik = sum_small(loglik) / total_people
    return (moved, log_weights[0], mean_loglik[0])


def solution(mesh):
    placed = (P("row", "col"), P("row"), P(None, "col"), P(None, None, "col"), P(), P(), P(), P())
    return jax.shard_map(
        local, mesh=mesh, in_specs=placed, out_specs=(P(None, "col"), P(), P()), check_vma=False
    )
```

```python
import functools

import jax
import jax.numpy as jnp
from jax import lax
from jax.experimental import pallas as pl
from jax.experimental.pallas import tpu as pltpu
from jax.sharding import PartitionSpec as P

CLIP_FLOOR = 4.0
SHRINKAGE_LEVEL = 0.5
F32 = jnp.float32
BF16 = jnp.bfloat16
VMEM = pl.BlockSpec(memory_space=pltpu.VMEM)
SMEM = pl.BlockSpec(memory_space=pltpu.SMEM)
HBM = pl.BlockSpec(memory_space=pltpu.HBM)
KEEP, SEND = 0, 1
MIB = 1 << 20
LANES = 128
LOW_FACTOR = 2048.0
CHUNKS = 1
PIECES = 4


def core_of():
    return lax.rem(lax.axis_index("col"), 2)


def row_bits():
    return [1 << b for b in range(lax.axis_size("row").bit_length() - 1)]


def half_of(which, piece, variants):
    columns = variants // PIECES
    bits = row_bits()
    bit = jnp.where(lax.rem(jnp.int32(piece), 2) == 0, bits[0], bits[-1])
    own = lax.rem(lax.div(lax.axis_index("row"), bit), 2)
    chosen = own if which == KEEP else 1 - own
    return pl.multiple_of(piece * columns + chosen * (columns // 2), columns // 2)


def rows_dot(left, right):
    return lax.dot_general(left, right, (((1,), (1,)), ((), ())), preferred_element_type=F32)


def tile_of(size, most):
    while size % most:
        most //= 2
    return most


def params(mib):
    return pltpu.CompilerParams(vmem_limit_bytes=mib * MIB)


def cost(flops):
    return pl.CostEstimate(flops=flops, bytes_accessed=0, transcendentals=0)


def as_lanes(value):
    high = value.astype(BF16)
    rest = value - high.astype(F32)
    middle = rest.astype(BF16)
    low = (rest - middle.astype(F32)).astype(BF16)
    lane = lax.broadcasted_iota(jnp.int32, (value.shape[0], LANES), 1)
    zero = jnp.zeros((value.shape[0], LANES), F32)
    out = jnp.where(lane == 0, high.astype(F32), zero)
    out = jnp.where(lane == 1, middle.astype(F32), out)
    return jnp.where(lane == 2, low.astype(F32), out).astype(BF16)


def flipped(value):
    size = max(value.shape)
    diagonal = lax.broadcasted_iota(jnp.int32, (size, size), 0) == lax.broadcasted_iota(
        jnp.int32, (size, size), 1
    )
    return jnp.sum(
        jnp.where(diagonal, value, 0.0), axis=int(value.shape[0] == 1), keepdims=True
    )


def from_lanes(lanes):
    return jnp.sum(lanes.astype(F32), axis=1, keepdims=True)


def center_kernel(block, scale, total_variants, doses, cloud, _, centered, mine, other, cloud_bf, logits, gram):
    step = pl.program_id(0)
    variants = doses.shape[1]
    people = logits.shape[1]
    half = people // 2

    @pl.when(step == 0)
    def _():
        cloud_bf[...] = cloud[...].astype(BF16)

    @pl.when(step == 0)
    def _():
        width = tile_of(variants, 1024)
        total = None
        for start in range(0, variants, width):
            c = cloud[:, start : start + width]
            c = c - jnp.mean(c, axis=0, keepdims=True)
            high = c.astype(BF16)
            low = (c - high.astype(F32)).astype(BF16)
            term = rows_dot(high, high) + 2.0 * rows_dot(high, low)
            total = term if total is None else total + term
        gram[...] = total * (1.0 / total_variants)

    width = tile_of(variants, 2048)
    total = None
    for start in range(0, variants, width):
        part = (doses[:, start : start + width] - 1).astype(F32).astype(BF16)
        centered[pl.ds(pl.multiple_of(step * block, block), block), start : start + width] = part
        term = rows_dot(part, cloud_bf[:, start : start + width])
        total = term if total is None else total + term
    logits[:, pl.ds(pl.multiple_of(step * block, block), block)] = total.T

    @pl.when(step == pl.num_programs(0) - 1)
    def _():
        first = core_of()
        for which, out in ((first, mine), (1 - first, other)):
            out[:, :half] = logits[:, pl.ds(pl.multiple_of(which * half, half), half)] * scale
            out[:, half : half + LANES // 2] = gram[...]
            out[:, half + LANES // 2 :] = gram[...]


def center_and_first_logits(scale, total_variants, doses, cloud, scalars):
    variants = doses.shape[1]
    people = doses.shape[0]
    particles = cloud.shape[0]
    block = min(256, people)
    steps = people // block
    exchanged = jax.ShapeDtypeStruct((particles, people // 2 + LANES), F32)
    return pl.pallas_call(
        functools.partial(center_kernel, block, scale, total_variants),
        grid=(steps,),
        in_specs=[
            pl.BlockSpec((block, variants), lambda i: (i, 0)),
            pl.BlockSpec((particles, variants), lambda i: (0, 0), pipeline_mode=pl.Buffered(1)),
            VMEM,
        ],
        out_specs=[VMEM, VMEM, VMEM],
        out_shape=[pltpu.VMEM((people, variants), BF16), exchanged, exchanged],
        scratch_shapes=[
            pltpu.VMEM((particles, variants), BF16),
            pltpu.VMEM((particles, people), F32),
            pltpu.VMEM((particles, particles), F32),
        ],
        compiler_params=params(28),
        cost_estimate=cost(16 * particles * people * variants),
        name="center_and_first_logits",
    )(doses, cloud, scalars)


def first_residual_kernel(status, values, out, gram):
    people = status.shape[1] // 2
    particles = gram.shape[0]
    logits = values[:, :people]
    outcome = outcome_of(status)
    out[:, :people] = (outcome - jax.nn.sigmoid(logits)).astype(BF16)
    out[:, people:] = as_lanes(loglik_of(outcome, logits))
    middle = people + LANES // 2
    gram[...] = values[:, people : people + particles] + values[:, middle : middle + particles] * (
        1.0 / LOW_FACTOR
    )


def first_residual_of(status, values):
    particles = values.shape[0]
    return pl.pallas_call(
        first_residual_kernel,
        in_specs=[VMEM, VMEM],
        out_specs=[VMEM, VMEM],
        out_shape=[
            jax.ShapeDtypeStruct(values.shape, BF16),
            jax.ShapeDtypeStruct((particles, particles), F32),
        ],
        compiler_params=params(8),
        name="first_residual",
    )(status, values)


def residual_kernel(scale, status, *refs):
    logits = tree_sum([ref[...].astype(F32) for ref in refs[:-1]]) * scale
    refs[-1][...] = (outcome_of(status) - jax.nn.sigmoid(logits)).astype(BF16)


def residual_of(scale, status, sent):
    return pl.pallas_call(
        functools.partial(residual_kernel, scale),
        in_specs=[VMEM] * (1 + len(sent)),
        out_specs=VMEM,
        out_shape=jax.ShapeDtypeStruct(sent[0].shape, BF16),
        compiler_params=params(8),
        name="residual",
    )(status, *sent)


def outcome_of(status):
    half = status.shape[1] // 2
    return status[:, pl.ds(pl.multiple_of(core_of() * half, half), half)].astype(F32)


def loglik_of(outcome, logits):
    softplus = jnp.maximum(logits, 0.0) + jnp.log1p(jnp.exp(-jnp.abs(logits)))
    return jnp.sum(outcome * logits - softplus, axis=1, keepdims=True)


def last_loglik_kernel(scale, status, *refs):
    logits = tree_sum([ref[...].astype(F32) for ref in refs[:-1]]) * scale
    refs[-1][...] = flipped(loglik_of(outcome_of(status), logits))


def last_loglik(scale, status, sent):
    return pl.pallas_call(
        functools.partial(last_loglik_kernel, scale),
        in_specs=[VMEM] * (1 + len(sent)),
        out_specs=VMEM,
        out_shape=jax.ShapeDtypeStruct((1, sent[0].shape[0]), F32),
        compiler_params=params(8),
        name="last_loglik",
    )(status, *sent)


def gradient_kernel(count, which, piece, tail, *refs):
    pairs, centered = refs[: 2 * count], refs[2 * count : 2 * count + CHUNKS]
    grad, residual = refs[2 * count + CHUNKS :]
    people, variants = centered[0].shape
    half = people // 2
    mine = core_of()
    for chunk in range(CHUNKS):
        own, other = (pairs[2 * chunk], pairs[2 * chunk + 1]) if count == CHUNKS else pairs
        at = 0 if count == CHUNKS else chunk * half
        base = chunk * people
        residual[:, pl.ds(pl.multiple_of(base + mine * half, half), half)] = own[:, at : at + half]
        residual[:, pl.ds(pl.multiple_of(base + (1 - mine) * half, half), half)] = other[
            :, at : at + half
        ]
    columns = variants // 2 // PIECES
    width = tile_of(columns, 512)
    first = half_of(which, piece, variants)
    for start in range(0, columns, width):
        grad[:, start : start + width] = sum(
            jnp.dot(
                residual[:, chunk * people : (chunk + 1) * people],
                centered[chunk][:, pl.ds(pl.multiple_of(first + start, width), width)],
                preferred_element_type=F32,
            )
            for chunk in range(CHUNKS)
        ).astype(BF16)
    if tail:
        grad[:, columns:] = as_lanes(from_lanes(own[:, half:]) + from_lanes(other[:, half:]))


def gradient(which, piece, pairs, centered, tail):
    particles = pairs[0].shape[0]
    people = sum(c.shape[0] for c in centered)
    columns = centered[0].shape[1] // 2 // PIECES
    return pl.pallas_call(
        functools.partial(gradient_kernel, len(pairs) // 2, which, piece, tail),
        in_specs=[VMEM] * (len(pairs) + CHUNKS),
        out_specs=VMEM,
        out_shape=jax.ShapeDtypeStruct((particles, columns + (LANES if tail else 0)), BF16),
        scratch_shapes=[pltpu.VMEM((particles, people), BF16)],
        compiler_params=params(8),
        cost_estimate=cost(8 * particles * people * columns),
        name="gradient",
    )(*pairs, *centered)


def pair_sum_kernel(columns, tail, left, right, out):
    total = left[:, :columns].astype(F32) + right[:, :columns].astype(F32)
    out[:, :columns] = total.astype(BF16)
    if tail:
        out[:, columns:] = as_lanes(from_lanes(left[:, columns:]) + from_lanes(right[:, columns:]))


def pair_sum(columns, tail, left, right):
    return pl.pallas_call(
        functools.partial(pair_sum_kernel, columns, tail),
        in_specs=[VMEM, VMEM],
        out_specs=VMEM,
        out_shape=jax.ShapeDtypeStruct((left.shape[0], columns + (LANES if tail else 0)), BF16),
        compiler_params=params(8),
        name="pair_sum",
    )(left, right)


def weigh(heat_advance, loglik, gram):
    scaled = heat_advance * loglik
    clipped = jnp.maximum(scaled - jnp.max(scaled, axis=0, keepdims=True), -CLIP_FLOOR)
    log_weights = clipped - jnp.log(jnp.sum(jnp.exp(clipped), axis=0, keepdims=True))
    weights = jnp.exp(log_weights)
    particles = loglik.shape[0]
    gram = gram[:, :particles]
    diagonal = lax.broadcasted_iota(jnp.int32, gram.shape, 0) == lax.broadcasted_iota(
        jnp.int32, gram.shape, 1
    )
    square = jnp.sum(jnp.where(diagonal, gram * weights, 0.0), axis=0, keepdims=True)
    mixed = jnp.sum(weights * gram, axis=0, keepdims=True) * flipped(weights)
    total = jnp.sum(square - mixed, axis=1, keepdims=True)
    return log_weights, weights, total + 1e-06


def update_kernel(which, move, total_variants, scalars, flags, noise, *refs):
    refs = list(refs)
    centered = [refs.pop(0) for _ in range(CHUNKS)]
    grads = [refs.pop(0) for _ in range(PIECES)]
    cloud = refs.pop(0)
    start_first, last = move == 0, move == 1
    people, variants = centered[0].shape
    columns = variants // 2
    advance = scalars[:, 1:2]
    heat = (scalars[:, 0:1] + advance) * float(total_variants) ** (-0.5)
    approved = flipped(flags[move : move + 1, :].astype(F32)) > 0.5
    if start_first and which == KEEP:
        gram, arrived, held = refs.pop(0), refs.pop(0), refs.pop(0)
    else:
        size_in = refs.pop(0)
    before = refs.pop(0) if which == SEND else None
    if last and which == SEND:
        refs.pop(0)
    moved = refs.pop(0)
    if start_first:
        if which == KEEP:
            sizes_out = (refs.pop(0), refs.pop(0))
            log_weights_out = refs.pop(0)
            loglik = from_lanes(held[:, columns // PIECES :]) + from_lanes(arrived[:, columns // PIECES :])
            log_weights, weights, mean_spread = weigh(advance, loglik, gram[...])
            log_weights_out[...] = flipped(log_weights)
            factor = scalars[:, 2:3] / mean_spread
            for half, size_out in enumerate(sizes_out):
                width = columns // PIECES
                narrow = tile_of(width, 512)
                for piece in range(PIECES):
                    begin = half_of(half, piece, variants)
                    for start in range(0, width, narrow):
                        there = pl.ds(pl.multiple_of(begin + start, narrow), narrow)
                        c = cloud[:, there]
                        center = jnp.sum(weights * c, axis=0, keepdims=True)
                        spread = jnp.sum(weights * (c - center) ** 2, axis=0, keepdims=True) + 1e-06
                        at = piece * width + start
                        size_out[:, at : at + narrow] = spread * factor
            size_in = sizes_out[KEEP]
    if which == KEEP:
        total = refs.pop(0)
    else:
        mine, other, total = refs.pop(0), refs.pop(0), refs.pop(0)
    if last:
        buffer, sems = refs
    copies = []
    width = tile_of(columns // PIECES, 2048)
    narrow = tile_of(width, 512)
    at_block = []
    for piece in range(PIECES):
        first = half_of(which, piece, variants)
        at_block += [first + start for start in range(0, columns // PIECES, width)]
    for block, first in enumerate(at_block):
        chosen = []
        for start in range(block * width, (block + 1) * width, narrow):
            there = pl.ds(pl.multiple_of(first + start - block * width, narrow), narrow)
            here = slice(start, start + narrow)
            c = cloud[:, there] if start_first else cloud[:, here]
            size = size_in[:, here]
            piece, at = divmod(start, columns // PIECES)
            slope = grads[piece][:, at : at + narrow].astype(F32)
            if last:
                c = c + jnp.where(approved, size * heat, 0.0) * slope
                buffer[:, here] = c
                chosen.append(c.astype(BF16))
                continue
            rise = heat * slope - SHRINKAGE_LEVEL * c * lax.rsqrt(c * c + 1.0)
            proposal = c + size * rise + jnp.sqrt(2.0 * size) * noise[move, :, there]
            c = jnp.where(approved, proposal, c)
            moved[:, here] = c
            chosen.append(c.astype(BF16))
        there = pl.ds(pl.multiple_of(first, width), width)
        if last:
            copies.append(
                pltpu.make_async_copy(
                    buffer.at[:, pl.ds(block * width, width)], moved.at[:, there], sems.at[block]
                )
            )
            copies[-1].start()
        chosen = jnp.concatenate(chosen, axis=1)
        for chunk in range(CHUNKS):
            rows = slice(chunk * people, (chunk + 1) * people)
            term = rows_dot(centered[chunk][:, there], chosen)
            if block > 0:
                term = total[rows, :] + term
            elif which == SEND:
                term = before[rows, :] + term
            total[rows, :] = term
    if which == SEND:
        half = people // 2
        here = core_of()
        for chunk in range(CHUNKS):
            out = slice(chunk * half, (chunk + 1) * half)
            base = chunk * people
            mine[:, out] = total[pl.ds(pl.multiple_of(base + here * half, half), half), :].T
            other[:, out] = total[pl.ds(pl.multiple_of(base + (1 - here) * half, half), half), :].T
    for copy in copies:
        copy.wait()


def drift_kernel(which, move, flags, noise, cloud, size_in, out):
    variants = noise.shape[2]
    columns = variants // 2
    width = columns // PIECES
    narrow = tile_of(width, 512)
    approved = flipped(flags[move : move + 1, :].astype(F32)) > 0.5
    for piece in range(PIECES):
        first = half_of(which, piece, variants)
        for start in range(0, width, narrow):
            there = pl.ds(pl.multiple_of(first + start, narrow), narrow)
            here = slice(piece * width + start, piece * width + start + narrow)
            c, size = cloud[:, here], size_in[:, here]
            pull = SHRINKAGE_LEVEL * c * lax.rsqrt(c * c + 1.0)
            free = c - size * pull + jnp.sqrt(2.0 * size) * noise[move, :, there]
            out[:, here] = jnp.where(approved, free, c)


def drift(which, move, fixed, cloud, size):
    return pl.pallas_call(
        functools.partial(drift_kernel, which, move),
        in_specs=[VMEM] * 4,
        out_specs=VMEM,
        out_shape=jax.ShapeDtypeStruct(cloud.shape, F32),
        compiler_params=params(8),
        name="drift",
    )(fixed[1], fixed[2], cloud, size)


def update(which, move, total_variants, fixed, centered, grads, cloud, extra, before, moved):
    flags = fixed[1]
    particles, variants = flags.shape[1], centered[0].shape[1]
    people = sum(c.shape[0] for c in centered)
    columns = variants // 2
    operands = [*fixed, *centered, *grads, cloud, *extra]
    if before is not None:
        operands.append(before)
    aliases = {}
    if moved is not None:
        aliases = {len(operands): 0}
        operands.append(moved)
    last = move == 1
    out_shape = [jax.ShapeDtypeStruct((particles, variants if last else columns), F32)]
    if not last:
        if which == KEEP:
            out_shape += [jax.ShapeDtypeStruct((1, columns), F32)] * 2
            out_shape.append(jax.ShapeDtypeStruct((1, particles), F32))
    scratch = []
    if which == KEEP:
        out_shape.append(jax.ShapeDtypeStruct((people, particles), F32))
    else:
        out_shape += [jax.ShapeDtypeStruct((particles, people // 2), F32)] * 2
        scratch.append(pltpu.VMEM((people, particles), F32))
    if last:
        blocks = columns // tile_of(columns // PIECES, 2048)
        scratch += [pltpu.VMEM((particles, columns), F32), pltpu.SemaphoreType.DMA((blocks,))]
    specs = [VMEM] * len(operands)
    if moved is not None:
        specs[-1] = HBM
    return pl.pallas_call(
        functools.partial(update_kernel, which, move, total_variants),
        in_specs=specs,
        out_specs=[HBM if last else VMEM] + [VMEM] * (len(out_shape) - 1),
        out_shape=out_shape,
        input_output_aliases=aliases,
        scratch_shapes=scratch,
        compiler_params=params(12),
        cost_estimate=cost(8 * particles * people * columns),
        name="update_and_logits",
    )(*operands)


def swap(value, axis, distance):
    size = lax.axis_size(axis)
    return lax.ppermute(value, axis, [(i, i ^ distance) for i in range(size)])


def tree_sum(values):
    values = list(values)
    while len(values) > 1:
        values = [values[i] + values[i + 1] for i in range(0, len(values), 2)]
    return values[0]


def after(value, earlier):
    return value if earlier is None else lax.optimization_barrier((value, earlier))[0]


def pair_sums(tails, held, arrived, width):
    sums = []
    for piece, tail in enumerate(tails):
        there = after(arrived[piece], sums[-1] if sums else None)
        sums.append(pair_sum(width, tail, held[piece], there))
    return sums


def swap_over_rows(value, piece, stage):
    rows, columns = lax.axis_size("row"), lax.axis_size("col")
    bits = row_bits()
    order = (bits[stage], bits[::-1][stage])
    return lax.ppermute(
        value,
        ("row", "col"),
        [
            (row * columns + col, (row ^ order[piece % 2]) * columns + col)
            for row in range(rows)
            for col in range(columns)
        ],
    )


def over_chips(mine):
    return [mine] + [swap(mine, "col", d) for d in range(2, lax.axis_size("col"), 2)]


def sum_small(value):
    value = value + swap(value, "col", 1)
    size = lax.axis_size("row")
    return tree_sum([value] + [swap(value, "row", d) for d in range(1, size)])


def local(
    allele_doses,
    disease_status,
    walker_cloud,
    normal_perturbations,
    approval_flags,
    present_heat,
    heat_advance,
    drift_magnitude,
):
    people, variants = allele_doses.shape
    total_variants = variants * lax.axis_size("col")
    total_people = people * lax.axis_size("row")
    scale = float(total_variants) ** (-0.5)
    status = disease_status.reshape(1, people)
    scalars = jnp.concatenate([present_heat, heat_advance, drift_magnitude])[None, :]

    part, mine, other = center_and_first_logits(
        scale, total_variants, allele_doses, walker_cloud, scalars
    )
    centered = [part]
    high, low = people // 2, people // 2 + LANES // 2
    values = mine + swap(other, "col", 1)
    lane = lax.broadcasted_iota(jnp.int32, values.shape, 1)
    rounded = lax.reduce_precision(values, exponent_bits=5, mantissa_bits=10)
    rest = (values - rounded) * LOW_FACTOR
    values = jnp.where(lane < high, values, jnp.where(lane < low, rounded, rest))
    sent = over_chips(values.astype(jnp.float16))
    own, gram = first_residual_of(status, tree_sum([each.astype(F32) for each in sent]))
    pairs = [own, swap(own, "col", 1)]

    width = variants // 2 // PIECES
    fixed = (scalars, approval_flags, normal_perturbations)
    stages = len(row_bits())
    pieces = range(PIECES)
    for move in range(2):
        first = move == 0
        tails = [first and piece == 0 for piece in pieces]
        sent_away = []
        for piece in pieces:
            there = after(pairs, sent_away[-1] if sent_away else None)
            sent_away.append(gradient(SEND, piece, there, centered, tails[piece]))
        arrived = [swap_over_rows(each, piece, 0) for piece, each in enumerate(sent_away)]
        for stage in range(1, stages):
            if stage == 1:
                held = []
                for piece in pieces:
                    there = after(pairs, held[piece - 2] if piece > 1 else sent_away[-1])
                    kept = gradient(KEEP, piece, there, centered, tails[piece])
                    there = after(arrived[piece], held[-1] if held else None)
                    held.append(pair_sum(width, tails[piece], kept, there))
            else:
                held = pair_sums(tails, held, arrived, width)
            arrived = [swap_over_rows(each, piece, stage) for piece, each in enumerate(held)]
        summed = pair_sums([False] * PIECES, held, arrived, width)
        arriving = [swap_over_rows(each, piece, 0) for piece, each in enumerate(summed)]
        if first:
            c_kept, size_kept, size_sent, log_weights, total = update(
                KEEP, move, total_variants, fixed, centered, summed, walker_cloud,
                [gram, arrived[0], held[0]], None, None,
            )
            c_sent, mine, other = update(
                SEND, move, total_variants, fixed, centered, arriving, walker_cloud,
                [size_sent], total, None,
            )
        else:
            moved, total = update(
                KEEP, move, total_variants, fixed, centered, summed, free_kept, [size_kept], None, None
            )
            moved, mine, other = update(
                SEND, move, total_variants, fixed, centered, arriving, free_sent, [size_sent], total, moved
            )
        sent = over_chips((mine + swap(other, "col", 1)).astype(BF16))
        if first:
            free_kept = drift(KEEP, 1, fixed, c_kept, size_kept)
            free_sent = drift(SEND, 1, fixed, c_sent, size_sent)
            (free_kept, free_sent), sent = lax.optimization_barrier(((free_kept, free_sent), sent))
            own = residual_of(scale, status, sent)
            pairs = [own, swap(own, "col", 1)]
    loglik = last_loglik(scale, status, sent)
    mean_loglik = sum_small(loglik) / total_people
    return (moved, log_weights[0], mean_loglik[0])


def solution(mesh):
    placed = (P("row", "col"), P("row"), P(None, "col"), P(None, None, "col"), P(), P(), P(), P())
    return jax.shard_map(
        local, mesh=mesh, in_specs=placed, out_specs=(P(None, "col"), P(), P()), check_vma=False
    )
```

```python
import functools

import jax
import jax.numpy as jnp
from jax import lax
from jax.experimental import pallas as pl
from jax.experimental.pallas import tpu as pltpu
from jax.sharding import PartitionSpec as P

CLIP_FLOOR = 4.0
SHRINKAGE_LEVEL = 0.5
F32 = jnp.float32
BF16 = jnp.bfloat16
VMEM = pl.BlockSpec(memory_space=pltpu.VMEM)
SMEM = pl.BlockSpec(memory_space=pltpu.SMEM)
HBM = pl.BlockSpec(memory_space=pltpu.HBM)
KEEP, SEND = 0, 1
MIB = 1 << 20
LANES = 128
LOW_FACTOR = 2048.0
CHUNKS = 1
PIECES = 4


def core_of():
    return lax.rem(lax.axis_index("col"), 2)


def row_bits():
    return [1 << b for b in range(lax.axis_size("row").bit_length() - 1)]


def half_of(which, piece, variants):
    columns = variants // PIECES
    bits = row_bits()
    bit = jnp.where(lax.rem(core_of() + piece, 2) == 0, bits[0], bits[-1])
    own = lax.rem(lax.div(lax.axis_index("row"), bit), 2)
    chosen = own if which == KEEP else 1 - own
    return pl.multiple_of(piece * columns + chosen * (columns // 2), columns // 2)


def rows_dot(left, right):
    return lax.dot_general(left, right, (((1,), (1,)), ((), ())), preferred_element_type=F32)


def tile_of(size, most):
    while size % most:
        most //= 2
    return most


def params(mib):
    return pltpu.CompilerParams(vmem_limit_bytes=mib * MIB)


def cost(flops):
    return pl.CostEstimate(flops=flops, bytes_accessed=0, transcendentals=0)


def as_lanes(value):
    high = value.astype(BF16)
    rest = value - high.astype(F32)
    middle = rest.astype(BF16)
    low = (rest - middle.astype(F32)).astype(BF16)
    lane = lax.broadcasted_iota(jnp.int32, (value.shape[0], LANES), 1)
    zero = jnp.zeros((value.shape[0], LANES), F32)
    out = jnp.where(lane == 0, high.astype(F32), zero)
    out = jnp.where(lane == 1, middle.astype(F32), out)
    return jnp.where(lane == 2, low.astype(F32), out).astype(BF16)


def flipped(value):
    size = max(value.shape)
    diagonal = lax.broadcasted_iota(jnp.int32, (size, size), 0) == lax.broadcasted_iota(
        jnp.int32, (size, size), 1
    )
    return jnp.sum(
        jnp.where(diagonal, value, 0.0), axis=int(value.shape[0] == 1), keepdims=True
    )


def from_lanes(lanes):
    return jnp.sum(lanes.astype(F32), axis=1, keepdims=True)


def center_kernel(block, scale, total_variants, doses, cloud, _, centered, mine, other, cloud_bf, logits, gram):
    step = pl.program_id(0)
    variants = doses.shape[1]
    people = logits.shape[1]
    half = people // 2

    @pl.when(step == 0)
    def _():
        cloud_bf[...] = cloud[...].astype(BF16)

    @pl.when(step == 0)
    def _():
        width = tile_of(variants, 1024)
        total = None
        for start in range(0, variants, width):
            c = cloud[:, start : start + width]
            c = c - jnp.mean(c, axis=0, keepdims=True)
            high = c.astype(BF16)
            low = (c - high.astype(F32)).astype(BF16)
            term = rows_dot(high, high) + 2.0 * rows_dot(high, low)
            total = term if total is None else total + term
        gram[...] = total * (1.0 / total_variants)

    width = tile_of(variants, 2048)
    total = None
    for start in range(0, variants, width):
        part = (doses[:, start : start + width] - 1).astype(F32).astype(BF16)
        centered[pl.ds(pl.multiple_of(step * block, block), block), start : start + width] = part
        term = rows_dot(part, cloud_bf[:, start : start + width])
        total = term if total is None else total + term
    logits[:, pl.ds(pl.multiple_of(step * block, block), block)] = total.T

    @pl.when(step == pl.num_programs(0) - 1)
    def _():
        first = core_of()
        for which, out in ((first, mine), (1 - first, other)):
            out[:, :half] = logits[:, pl.ds(pl.multiple_of(which * half, half), half)] * scale
            out[:, half : half + LANES // 2] = gram[...]
            out[:, half + LANES // 2 :] = gram[...]


def center_and_first_logits(scale, total_variants, doses, cloud, scalars):
    variants = doses.shape[1]
    people = doses.shape[0]
    particles = cloud.shape[0]
    block = min(256, people)
    steps = people // block
    exchanged = jax.ShapeDtypeStruct((particles, people // 2 + LANES), F32)
    return pl.pallas_call(
        functools.partial(center_kernel, block, scale, total_variants),
        grid=(steps,),
        in_specs=[
            pl.BlockSpec((block, variants), lambda i: (i, 0)),
            pl.BlockSpec((particles, variants), lambda i: (0, 0), pipeline_mode=pl.Buffered(1)),
            VMEM,
        ],
        out_specs=[VMEM, VMEM, VMEM],
        out_shape=[pltpu.VMEM((people, variants), BF16), exchanged, exchanged],
        scratch_shapes=[
            pltpu.VMEM((particles, variants), BF16),
            pltpu.VMEM((particles, people), F32),
            pltpu.VMEM((particles, particles), F32),
        ],
        compiler_params=params(28),
        cost_estimate=cost(16 * particles * people * variants),
        name="center_and_first_logits",
    )(doses, cloud, scalars)


def first_residual_kernel(status, values, out, gram):
    people = status.shape[1] // 2
    particles = gram.shape[0]
    logits = values[:, :people]
    outcome = outcome_of(status)
    out[:, :people] = (outcome - jax.nn.sigmoid(logits)).astype(BF16)
    out[:, people:] = as_lanes(loglik_of(outcome, logits))
    middle = people + LANES // 2
    gram[...] = values[:, people : people + particles] + values[:, middle : middle + particles] * (
        1.0 / LOW_FACTOR
    )


def first_residual_of(status, values):
    particles = values.shape[0]
    return pl.pallas_call(
        first_residual_kernel,
        in_specs=[VMEM, VMEM],
        out_specs=[VMEM, VMEM],
        out_shape=[
            jax.ShapeDtypeStruct(values.shape, BF16),
            jax.ShapeDtypeStruct((particles, particles), F32),
        ],
        compiler_params=params(8),
        name="first_residual",
    )(status, values)


def residual_kernel(scale, status, *refs):
    logits = tree_sum([ref[...].astype(F32) for ref in refs[:-1]]) * scale
    refs[-1][...] = (outcome_of(status) - jax.nn.sigmoid(logits)).astype(BF16)


def residual_of(scale, status, sent):
    return pl.pallas_call(
        functools.partial(residual_kernel, scale),
        in_specs=[VMEM] * (1 + len(sent)),
        out_specs=VMEM,
        out_shape=jax.ShapeDtypeStruct(sent[0].shape, BF16),
        compiler_params=params(8),
        name="residual",
    )(status, *sent)


def outcome_of(status):
    half = status.shape[1] // 2
    return status[:, pl.ds(pl.multiple_of(core_of() * half, half), half)].astype(F32)


def loglik_of(outcome, logits):
    softplus = jnp.maximum(logits, 0.0) + jnp.log1p(jnp.exp(-jnp.abs(logits)))
    return jnp.sum(outcome * logits - softplus, axis=1, keepdims=True)


def last_loglik_kernel(scale, status, *refs):
    logits = tree_sum([ref[...].astype(F32) for ref in refs[:-1]]) * scale
    refs[-1][...] = flipped(loglik_of(outcome_of(status), logits))


def last_loglik(scale, status, sent):
    return pl.pallas_call(
        functools.partial(last_loglik_kernel, scale),
        in_specs=[VMEM] * (1 + len(sent)),
        out_specs=VMEM,
        out_shape=jax.ShapeDtypeStruct((1, sent[0].shape[0]), F32),
        compiler_params=params(8),
        name="last_loglik",
    )(status, *sent)


def gradient_kernel(count, which, piece, tail, *refs):
    pairs, centered = refs[: 2 * count], refs[2 * count : 2 * count + CHUNKS]
    grad, residual = refs[2 * count + CHUNKS :]
    people, variants = centered[0].shape
    half = people // 2
    mine = core_of()
    for chunk in range(CHUNKS):
        own, other = (pairs[2 * chunk], pairs[2 * chunk + 1]) if count == CHUNKS else pairs
        at = 0 if count == CHUNKS else chunk * half
        base = chunk * people
        residual[:, pl.ds(pl.multiple_of(base + mine * half, half), half)] = own[:, at : at + half]
        residual[:, pl.ds(pl.multiple_of(base + (1 - mine) * half, half), half)] = other[
            :, at : at + half
        ]
    columns = variants // 2 // PIECES
    width = tile_of(columns, 512)
    first = half_of(which, piece, variants)
    for start in range(0, columns, width):
        grad[:, start : start + width] = sum(
            jnp.dot(
                residual[:, chunk * people : (chunk + 1) * people],
                centered[chunk][:, pl.ds(pl.multiple_of(first + start, width), width)],
                preferred_element_type=F32,
            )
            for chunk in range(CHUNKS)
        ).astype(BF16)
    if tail:
        grad[:, columns:] = as_lanes(from_lanes(own[:, half:]) + from_lanes(other[:, half:]))


def gradient(which, piece, pairs, centered, tail):
    particles = pairs[0].shape[0]
    people = sum(c.shape[0] for c in centered)
    columns = centered[0].shape[1] // 2 // PIECES
    return pl.pallas_call(
        functools.partial(gradient_kernel, len(pairs) // 2, which, piece, tail),
        in_specs=[VMEM] * (len(pairs) + CHUNKS),
        out_specs=VMEM,
        out_shape=jax.ShapeDtypeStruct((particles, columns + (LANES if tail else 0)), BF16),
        scratch_shapes=[pltpu.VMEM((particles, people), BF16)],
        compiler_params=params(8),
        cost_estimate=cost(8 * particles * people * columns),
        name="gradient",
    )(*pairs, *centered)


def pair_sum_kernel(columns, tail, left, right, out):
    total = left[:, :columns].astype(F32) + right[:, :columns].astype(F32)
    out[:, :columns] = total.astype(BF16)
    if tail:
        out[:, columns:] = as_lanes(from_lanes(left[:, columns:]) + from_lanes(right[:, columns:]))


def pair_sum(columns, tail, left, right):
    return pl.pallas_call(
        functools.partial(pair_sum_kernel, columns, tail),
        in_specs=[VMEM, VMEM],
        out_specs=VMEM,
        out_shape=jax.ShapeDtypeStruct((left.shape[0], columns + (LANES if tail else 0)), BF16),
        compiler_params=params(8),
        name="pair_sum",
    )(left, right)


def weigh(heat_advance, loglik, gram):
    scaled = heat_advance * loglik
    clipped = jnp.maximum(scaled - jnp.max(scaled, axis=0, keepdims=True), -CLIP_FLOOR)
    log_weights = clipped - jnp.log(jnp.sum(jnp.exp(clipped), axis=0, keepdims=True))
    weights = jnp.exp(log_weights)
    particles = loglik.shape[0]
    gram = gram[:, :particles]
    diagonal = lax.broadcasted_iota(jnp.int32, gram.shape, 0) == lax.broadcasted_iota(
        jnp.int32, gram.shape, 1
    )
    square = jnp.sum(jnp.where(diagonal, gram * weights, 0.0), axis=0, keepdims=True)
    mixed = jnp.sum(weights * gram, axis=0, keepdims=True) * flipped(weights)
    total = jnp.sum(square - mixed, axis=1, keepdims=True)
    return log_weights, weights, total + 1e-06


def update_kernel(which, move, total_variants, scalars, flags, noise, *refs):
    refs = list(refs)
    centered = [refs.pop(0) for _ in range(CHUNKS)]
    grads = [refs.pop(0) for _ in range(PIECES)]
    cloud = refs.pop(0)
    start_first, last = move == 0, move == 1
    people, variants = centered[0].shape
    columns = variants // 2
    advance = scalars[:, 1:2]
    heat = (scalars[:, 0:1] + advance) * float(total_variants) ** (-0.5)
    approved = flipped(flags[move : move + 1, :].astype(F32)) > 0.5
    if start_first and which == KEEP:
        gram, arrived, held = refs.pop(0), refs.pop(0), refs.pop(0)
    else:
        size_in = refs.pop(0)
    before = refs.pop(0) if which == SEND else None
    if last and which == SEND:
        refs.pop(0)
    moved = refs.pop(0)
    if start_first:
        if which == KEEP:
            sizes_out = (refs.pop(0), refs.pop(0))
            log_weights_out = refs.pop(0)
            loglik = from_lanes(held[:, columns // PIECES :]) + from_lanes(arrived[:, columns // PIECES :])
            log_weights, weights, mean_spread = weigh(advance, loglik, gram[...])
            log_weights_out[...] = flipped(log_weights)
            factor = scalars[:, 2:3] / mean_spread
            for half, size_out in enumerate(sizes_out):
                width = columns // PIECES
                narrow = tile_of(width, 512)
                for piece in range(PIECES):
                    begin = half_of(half, piece, variants)
                    for start in range(0, width, narrow):
                        there = pl.ds(pl.multiple_of(begin + start, narrow), narrow)
                        c = cloud[:, there]
                        center = jnp.sum(weights * c, axis=0, keepdims=True)
                        spread = jnp.sum(weights * (c - center) ** 2, axis=0, keepdims=True) + 1e-06
                        at = piece * width + start
                        size_out[:, at : at + narrow] = spread * factor
            size_in = sizes_out[KEEP]
    if which == KEEP:
        total = refs.pop(0)
    else:
        mine, other, total = refs.pop(0), refs.pop(0), refs.pop(0)
    if last:
        buffer, sems = refs
    copies = []
    width = tile_of(columns // PIECES, 2048)
    narrow = tile_of(width, 512)
    at_block = []
    for piece in range(PIECES):
        first = half_of(which, piece, variants)
        at_block += [first + start for start in range(0, columns // PIECES, width)]
    for block, first in enumerate(at_block):
        chosen = []
        for start in range(block * width, (block + 1) * width, narrow):
            there = pl.ds(pl.multiple_of(first + start - block * width, narrow), narrow)
            here = slice(start, start + narrow)
            c = cloud[:, there] if start_first else cloud[:, here]
            size = size_in[:, here]
            piece, at = divmod(start, columns // PIECES)
            slope = grads[piece][:, at : at + narrow].astype(F32)
            if last:
                c = c + jnp.where(approved, size * heat, 0.0) * slope
                buffer[:, here] = c
                chosen.append(c.astype(BF16))
                continue
            rise = heat * slope - SHRINKAGE_LEVEL * c * lax.rsqrt(c * c + 1.0)
            proposal = c + size * rise + jnp.sqrt(2.0 * size) * noise[move, :, there]
            c = jnp.where(approved, proposal, c)
            moved[:, here] = c
            chosen.append(c.astype(BF16))
        there = pl.ds(pl.multiple_of(first, width), width)
        if last:
            copies.append(
                pltpu.make_async_copy(
                    buffer.at[:, pl.ds(block * width, width)], moved.at[:, there], sems.at[block]
                )
            )
            copies[-1].start()
        chosen = jnp.concatenate(chosen, axis=1)
        for chunk in range(CHUNKS):
            rows = slice(chunk * people, (chunk + 1) * people)
            term = rows_dot(centered[chunk][:, there], chosen)
            if block > 0:
                term = total[rows, :] + term
            elif which == SEND:
                term = before[rows, :] + term
            total[rows, :] = term
    if which == SEND:
        half = people // 2
        here = core_of()
        for chunk in range(CHUNKS):
            out = slice(chunk * half, (chunk + 1) * half)
            base = chunk * people
            mine[:, out] = total[pl.ds(pl.multiple_of(base + here * half, half), half), :].T
            other[:, out] = total[pl.ds(pl.multiple_of(base + (1 - here) * half, half), half), :].T
    for copy in copies:
        copy.wait()


def drift_kernel(which, move, flags, noise, cloud, size_in, out):
    variants = noise.shape[2]
    columns = variants // 2
    width = columns // PIECES
    narrow = tile_of(width, 512)
    approved = flipped(flags[move : move + 1, :].astype(F32)) > 0.5
    for piece in range(PIECES):
        first = half_of(which, piece, variants)
        for start in range(0, width, narrow):
            there = pl.ds(pl.multiple_of(first + start, narrow), narrow)
            here = slice(piece * width + start, piece * width + start + narrow)
            c, size = cloud[:, here], size_in[:, here]
            pull = SHRINKAGE_LEVEL * c * lax.rsqrt(c * c + 1.0)
            free = c - size * pull + jnp.sqrt(2.0 * size) * noise[move, :, there]
            out[:, here] = jnp.where(approved, free, c)


def drift(which, move, fixed, cloud, size):
    return pl.pallas_call(
        functools.partial(drift_kernel, which, move),
        in_specs=[VMEM] * 4,
        out_specs=VMEM,
        out_shape=jax.ShapeDtypeStruct(cloud.shape, F32),
        compiler_params=params(8),
        name="drift",
    )(fixed[1], fixed[2], cloud, size)


def update(which, move, total_variants, fixed, centered, grads, cloud, extra, before, moved):
    flags = fixed[1]
    particles, variants = flags.shape[1], centered[0].shape[1]
    people = sum(c.shape[0] for c in centered)
    columns = variants // 2
    operands = [*fixed, *centered, *grads, cloud, *extra]
    if before is not None:
        operands.append(before)
    aliases = {}
    if moved is not None:
        aliases = {len(operands): 0}
        operands.append(moved)
    last = move == 1
    out_shape = [jax.ShapeDtypeStruct((particles, variants if last else columns), F32)]
    if not last:
        if which == KEEP:
            out_shape += [jax.ShapeDtypeStruct((1, columns), F32)] * 2
            out_shape.append(jax.ShapeDtypeStruct((1, particles), F32))
    scratch = []
    if which == KEEP:
        out_shape.append(jax.ShapeDtypeStruct((people, particles), F32))
    else:
        out_shape += [jax.ShapeDtypeStruct((particles, people // 2), F32)] * 2
        scratch.append(pltpu.VMEM((people, particles), F32))
    if last:
        blocks = columns // tile_of(columns // PIECES, 2048)
        scratch += [pltpu.VMEM((particles, columns), F32), pltpu.SemaphoreType.DMA((blocks,))]
    specs = [VMEM] * len(operands)
    if moved is not None:
        specs[-1] = HBM
    return pl.pallas_call(
        functools.partial(update_kernel, which, move, total_variants),
        in_specs=specs,
        out_specs=[HBM if last else VMEM] + [VMEM] * (len(out_shape) - 1),
        out_shape=out_shape,
        input_output_aliases=aliases,
        scratch_shapes=scratch,
        compiler_params=params(12),
        cost_estimate=cost(8 * particles * people * columns),
        name="update_and_logits",
    )(*operands)


def swap(value, axis, distance):
    size = lax.axis_size(axis)
    return lax.ppermute(value, axis, [(i, i ^ distance) for i in range(size)])


def tree_sum(values):
    values = list(values)
    while len(values) > 1:
        values = [values[i] + values[i + 1] for i in range(0, len(values), 2)]
    return values[0]


def after(value, earlier):
    return value if earlier is None else lax.optimization_barrier((value, earlier))[0]


def pair_sums(tails, held, arrived, width):
    sums = []
    for piece, tail in enumerate(tails):
        there = after(arrived[piece], sums[-1] if sums else None)
        sums.append(pair_sum(width, tail, held[piece], there))
    return sums


def swap_over_rows(value, piece, stage):
    rows, columns = lax.axis_size("row"), lax.axis_size("col")
    bits = row_bits()
    order = (bits[stage], bits[::-1][stage])
    return lax.ppermute(
        value,
        ("row", "col"),
        [
            (row * columns + col, (row ^ order[(col + piece) % 2]) * columns + col)
            for row in range(rows)
            for col in range(columns)
        ],
    )


def over_chips(mine):
    return [mine] + [swap(mine, "col", d) for d in range(2, lax.axis_size("col"), 2)]


def sum_small(value):
    value = value + swap(value, "col", 1)
    size = lax.axis_size("row")
    return tree_sum([value] + [swap(value, "row", d) for d in range(1, size)])


def local(
    allele_doses,
    disease_status,
    walker_cloud,
    normal_perturbations,
    approval_flags,
    present_heat,
    heat_advance,
    drift_magnitude,
):
    people, variants = allele_doses.shape
    total_variants = variants * lax.axis_size("col")
    total_people = people * lax.axis_size("row")
    scale = float(total_variants) ** (-0.5)
    status = disease_status.reshape(1, people)
    scalars = jnp.concatenate([present_heat, heat_advance, drift_magnitude])[None, :]

    part, mine, other = center_and_first_logits(
        scale, total_variants, allele_doses, walker_cloud, scalars
    )
    centered = [part]
    high, low = people // 2, people // 2 + LANES // 2
    values = mine + swap(other, "col", 1)
    lane = lax.broadcasted_iota(jnp.int32, values.shape, 1)
    rounded = lax.reduce_precision(values, exponent_bits=5, mantissa_bits=10)
    rest = (values - rounded) * LOW_FACTOR
    values = jnp.where(lane < high, values, jnp.where(lane < low, rounded, rest))
    sent = over_chips(values.astype(jnp.float16))
    own, gram = first_residual_of(status, tree_sum([each.astype(F32) for each in sent]))
    pairs = [own, swap(own, "col", 1)]

    width = variants // 2 // PIECES
    fixed = (scalars, approval_flags, normal_perturbations)
    stages = len(row_bits())
    pieces = range(PIECES)
    for move in range(2):
        first = move == 0
        tails = [first and piece == 0 for piece in pieces]
        sent_away = []
        for piece in pieces:
            there = after(pairs, sent_away[-1] if sent_away else None)
            sent_away.append(gradient(SEND, piece, there, centered, tails[piece]))
        arrived = [swap_over_rows(each, piece, 0) for piece, each in enumerate(sent_away)]
        for stage in range(1, stages):
            if stage == 1:
                held = []
                for piece in pieces:
                    there = after(pairs, held[piece - 2] if piece > 1 else sent_away[-1])
                    kept = gradient(KEEP, piece, there, centered, tails[piece])
                    there = after(arrived[piece], held[-1] if held else None)
                    held.append(pair_sum(width, tails[piece], kept, there))
            else:
                held = pair_sums(tails, held, arrived, width)
            arrived = [swap_over_rows(each, piece, stage) for piece, each in enumerate(held)]
        summed = pair_sums([False] * PIECES, held, arrived, width)
        arriving = [swap_over_rows(each, piece, 0) for piece, each in enumerate(summed)]
        if first:
            c_kept, size_kept, size_sent, log_weights, total = update(
                KEEP, move, total_variants, fixed, centered, summed, walker_cloud,
                [gram, arrived[0], held[0]], None, None,
            )
            c_sent, mine, other = update(
                SEND, move, total_variants, fixed, centered, arriving, walker_cloud,
                [size_sent], total, None,
            )
        else:
            moved, total = update(
                KEEP, move, total_variants, fixed, centered, summed, free_kept, [size_kept], None, None
            )
            moved, mine, other = update(
                SEND, move, total_variants, fixed, centered, arriving, free_sent, [size_sent], total, moved
            )
        sent = over_chips((mine + swap(other, "col", 1)).astype(BF16))
        if first:
            free_kept = drift(KEEP, 1, fixed, c_kept, size_kept)
            free_sent = drift(SEND, 1, fixed, c_sent, size_sent)
            (free_kept, free_sent), sent = lax.optimization_barrier(((free_kept, free_sent), sent))
            own = residual_of(scale, status, sent)
            pairs = [own, swap(own, "col", 1)]
    loglik = last_loglik(scale, status, sent)
    mean_loglik = sum_small(loglik) / total_people
    return (moved, log_weights[0], mean_loglik[0])


def solution(mesh):
    placed = (P("row", "col"), P("row"), P(None, "col"), P(None, None, "col"), P(), P(), P(), P())
    return jax.shard_map(
        local, mesh=mesh, in_specs=placed, out_specs=(P(None, "col"), P(), P()), check_vma=False
    )
```
